512 devices in a mesh: dp: 128 (over x, z, core), mp: 4 (over y).
Axes of the slice: x: 4, y: 4, z: 16, core: 2. Of those that a mesh axis runs over, the one named last changes fastest.
Arguments:
- patches: bfloat16 [32768, 1280], P('dp', 'mp'), may hold values from -6 to 6
- routes: int32 [32768, 1], P('dp'), may hold values from 0 to 127; in each aligned block of 256 rows (0 to 255, 256 to 511, ...) at most 4 rows name the same one
- gain: bfloat16 [1280], replicated, may hold values from 0.099609375 to 1.8984375
- shift: bfloat16 [1280], replicated, may hold values from -2 to 2
- first_weight: bfloat16 [1280, 5120], P('dp', 'mp'), may hold values from -0.15625 to 0.15625
- first_bias: bfloat16 [5120], P('mp'), may hold values from -3 to 3
- adapter_down: bfloat16 [1280, 64], replicated, may hold values from -0.15625 to 0.15625
- adapter_up: bfloat16 [64, 5120], P(None, 'mp'), may hold values from -0.75 to 0.75
- second_weight: bfloat16 [5120, 1280], P('mp', 'dp'), may hold values from -0.078125 to 0.078125
- second_bias: bfloat16 [1280], P('mp'), may hold values from -3 to 3
- language_slot_gradient: bfloat16 [65536, 1280], P('dp', 'mp'), may hold values from -6 to 6
Outputs:
- embeds_llm: bfloat16 [65536, 1280], P('dp', 'mp')
- grad_lora_a: float32 [1280, 64], replicated
- grad_lora_b: float32 [64, 5120], P(None, 'mp')
The draws below stay inside these ranges and needn't reach their ends.
Inputs may be any that keep to these rules, and one draw needn't show every extreme that they name: `routes`: among the rows of one data rank, no destination is named more than 4 times, a bound that some block reaches.
All inputs are finite; a program needn't handle non-finite values.
Results may differ from the reference program's by a relative error of at most 0.012.
Values may be sent and summed in bfloat16 or wider, within the bound.
A program may use at most 64 MiB of HBM per device.

```python
import math
import jax
import jax.numpy as jnp
import numpy as np
from jax import lax

ENCODER_WIDTH = 1280
HIDDEN_UNITS = 5120
ADAPTER_RANK = 64
P_DEV = 256
CAP = 4
TOKENS = 32768
SLOTS = 65536
N_DP = 128
N_MP = 4


def level_of(key, shape, cuts, low, top_value):
    factor_of, own = 1.0, jax.random.fold_in(key, 6)
    for axis_at, shards_of in cuts:
        heights = jnp.exp(jax.random.uniform(jax.random.fold_in(own, axis_at), (shards_of,), jnp.float32, low / len(cuts), top_value / len(cuts)))
        factor_of = factor_of * jnp.repeat(heights, shape[axis_at] // shards_of).reshape([-1 if axis == axis_at else 1 for axis in range(len(shape))])
    return factor_of


def assign_block(own_key, own, number, rows, count, top, limit, lean):
    order = jax.random.permutation(own_key, count)
    packed, usual = shares(count, rows * top, limit, lean, True), shares(count, rows * top, limit, lean, False)
    places = jnp.arange(count)

    def named(tallies, offset_by):
        used = int((tallies > 0).sum())
        fixed = max(1, used // 4)
        shifted = fixed + (places - fixed + offset_by * (used - fixed)) % max(1, count - fixed)
        return jnp.zeros((count,), jnp.int32).at[order[jnp.where(places < fixed, places, shifted)]].set(jnp.asarray(tallies, jnp.int32))

    tallies = jnp.where(number % 4 == 0, named(packed, number // 4), named(usual, number - number // 4 - 1))
    mixed = jax.random.permutation(jax.random.fold_in(own, 3), count)
    source_of, taker = mixed[0:count // 2 * 2:2], mixed[1:count // 2 * 2:2]
    margin = jnp.minimum(tallies[source_of] - 1, limit - tallies[taker]) // 2
    margin = jnp.where((source_of == order[0]) | (taker == order[0]) | (tallies[taker] == 0), 0, jnp.maximum(margin, 0))
    shifted = jax.random.randint(jax.random.fold_in(own, 4), (count // 2,), 0, 1 << 20) % (margin + 1)
    tallies = tallies.at[source_of].add(-shifted).at[taker].add(shifted)
    items = jnp.searchsorted(jnp.cumsum(tallies), jnp.arange(rows * top), side="right").astype(jnp.int32)
    table = items.reshape(top, rows).T
    table = table[jax.random.permutation(jax.random.fold_in(own, 1), rows)]
    offset_by = jax.random.randint(jax.random.fold_in(own, 2), (rows, 1), 0, top)
    return jnp.take_along_axis(table, (jnp.arange(top)[None, :] + offset_by) % top, axis=1)


def shares(number_of, total, most, slope, full):
    portions = [(1 << 20) // math.isqrt(rank ** slope) + 1 for rank in range(1, number_of + 1)]
    largest = most if full else min(most, max(-(-total // number_of), total * portions[0] // sum(portions)))
    least = 1 if total - largest >= number_of - 1 else 0
    given, rest = [largest] + [least] * (number_of - 1), total - largest - least * (number_of - 1)
    while rest > 0:
        free = [i for i in range(1, number_of) if given[i] < largest] or [i for i in range(1, number_of) if given[i] < most]
        pool, remaining = sum([portions[i] for i in free]), rest
        for i in free:
            extra = min(most - given[i], max(1, remaining * portions[i] // pool), rest)
            given[i] = given[i] + extra
            rest = rest - extra
    return np.array(given)


def bell_draw(own_key, dims, scale, most, split=(), kind=jnp.bfloat16):
    result = scale * jax.random.normal(own_key, dims, jnp.float32)
    if split:
        result = result * level_of(own_key, dims, split, -0.22, 0.18)
    return jnp.clip(result, -most, most).astype(kind)


def setup_inputs(seed: int = 0) -> dict:
    splits = jax.random.split(jax.random.key(seed), 12)
    patches = bell_draw(splits[0], (TOKENS, ENCODER_WIDTH), 1.0, 6.0, ((0, 128), (1, 4)))
    routes_keys = jax.random.split(jax.random.fold_in(splits[1], 1), TOKENS // P_DEV)
    routes_turns = jax.random.permutation(jax.random.fold_in(splits[1], 3), TOKENS // P_DEV)
    routes = jax.vmap(lambda own, number: assign_block(jax.random.fold_in(splits[1], 2), own, number, P_DEV, N_DP, 1, CAP, 2))(routes_keys, routes_turns).reshape((TOKENS, 1))
    gain = jnp.clip(1.0 + 0.18 * jax.random.normal(splits[2], (ENCODER_WIDTH,), jnp.float32), 0.099609375, 1.8984375).astype(jnp.bfloat16)
    shift = bell_draw(splits[3], (ENCODER_WIDTH,), 0.4, 2.0)
    first_weight = bell_draw(splits[4], (ENCODER_WIDTH, HIDDEN_UNITS), ENCODER_WIDTH ** -0.5, 0.15625, ((0, 128), (1, 4)))
    first_bias = bell_draw(splits[5], (HIDDEN_UNITS,), 0.5, 3.0, ((0, 4),))
    adapter_down = bell_draw(splits[6], (ENCODER_WIDTH, ADAPTER_RANK), ENCODER_WIDTH ** -0.5, 0.15625)
    adapter_up = bell_draw(splits[7], (ADAPTER_RANK, HIDDEN_UNITS), ADAPTER_RANK ** -0.5, 0.75, ((1, 4),))
    second_weight = bell_draw(splits[8], (HIDDEN_UNITS, ENCODER_WIDTH), HIDDEN_UNITS ** -0.5, 0.078125, ((0, 4), (1, 128)))
    second_bias = bell_draw(splits[9], (ENCODER_WIDTH,), 0.5, 3.0, ((0, 4),))
    language_slot_gradient = bell_draw(splits[10], (SLOTS, ENCODER_WIDTH), 1.0, 6.0, ((0, 128), (1, 4)))
    return {"patches": patches, "routes": routes, "gain": gain, "shift": shift, "first_weight": first_weight, "first_bias": first_bias, "adapter_down": adapter_down, "adapter_up": adapter_up, "second_weight": second_weight, "second_bias": second_bias, "language_slot_gradient": language_slot_gradient}


def quick_gelu(values):
    return values * jax.nn.sigmoid(1.702 * values)

def gelu_slope(values):
    sigma = jax.nn.sigmoid(1.702 * values)
    return sigma + 1.702 * values * sigma * (1.0 - sigma)

def normalize(patch_rows, gain, shift):
    floats = patch_rows.astype(jnp.float32)
    row_mean = lax.optimization_barrier(jnp.mean(floats, axis=-1, keepdims=True))
    centred = floats - row_mean
    row_var = lax.optimization_barrier(jnp.mean(centred * centred, axis=-1, keepdims=True))
    scaled = centred * lax.rsqrt(row_var + 1e-06) * gain.astype(jnp.float32) + shift.astype(jnp.float32)
    return scaled.astype(jnp.bfloat16)

def reference(patches, routes, gain, shift, first_weight, first_bias, adapter_down, adapter_up, second_weight, second_bias, language_slot_gradient):
    slots_rank = N_DP * CAP
    destination = routes[:, 0].reshape(N_DP, P_DEV)
    hit_table = (destination[:, :, None] == jnp.arange(N_DP, dtype=jnp.int32)[None, None, :]).astype(jnp.int32)
    before = jnp.cumsum(hit_table, axis=1) - hit_table
    rank_in = lax.optimization_barrier(jnp.sum(before * hit_table, axis=2))
    source = jnp.arange(N_DP, dtype=jnp.int32)[:, None]
    target = (destination * slots_rank + source * CAP + rank_in).reshape(-1).astype(jnp.int32)
    cotangent = language_slot_gradient[target]
    group = HIDDEN_UNITS // N_MP

    def one_block(loop_carry, inputs):
        patch_rows, grad_rows = inputs
        normalized_rows = normalize(patch_rows, gain, shift)
        adapter_latent = jnp.dot(normalized_rows, adapter_down, preferred_element_type=jnp.float32).astype(jnp.bfloat16)
        preactivation = jnp.dot(normalized_rows, first_weight, preferred_element_type=jnp.float32) + jnp.dot(adapter_latent, adapter_up, preferred_element_type=jnp.float32) + first_bias.astype(jnp.float32)
        activated = quick_gelu(preactivation).astype(jnp.bfloat16)
        pieces = jnp.einsum('rmf,mfd->rmd', activated.reshape(-1, N_MP, group).astype(jnp.float32), second_weight.reshape(N_MP, group, ENCODER_WIDTH).astype(jnp.float32))
        rounded = lax.optimization_barrier(pieces.astype(jnp.bfloat16))
        branch_out = lax.optimization_barrier(jnp.sum(rounded.astype(jnp.float32), axis=1))
        embeds = (patch_rows.astype(jnp.float32) + branch_out + second_bias.astype(jnp.float32)).astype(jnp.bfloat16)
        grad_act = jnp.dot(grad_rows, second_weight.T, preferred_element_type=jnp.float32)
        preactivation_gradient = (grad_act * gelu_slope(preactivation)).astype(jnp.bfloat16)
        adapter_gradient = jnp.dot(preactivation_gradient, adapter_up.T, preferred_element_type=jnp.float32)
        down_gradient = loop_carry[0] + jnp.dot(normalized_rows.astype(jnp.float32).T, adapter_gradient, precision=lax.Precision.HIGHEST)
        grad_b = loop_carry[1] + jnp.dot(adapter_latent.T, preactivation_gradient, preferred_element_type=jnp.float32)
        return ((down_gradient, grad_b), embeds)
    block_rows = TOKENS // 8
    start_index = (jnp.zeros((ENCODER_WIDTH, ADAPTER_RANK), jnp.float32), jnp.zeros((ADAPTER_RANK, HIDDEN_UNITS), jnp.float32))
    (down_gradient, grad_b), embeds = lax.scan(one_block, start_index, (patches.reshape(8, block_rows, ENCODER_WIDTH), cotangent.reshape(8, block_rows, ENCODER_WIDTH)))
    embeds = embeds.reshape(TOKENS, ENCODER_WIDTH)
    embeds_llm = jnp.zeros((N_DP * slots_rank, ENCODER_WIDTH), jnp.bfloat16).at[target].set(embeds)
    grad_scale = 1.0 / math.sqrt(TOKENS)
    return (embeds_llm, down_gradient * grad_scale, grad_b * grad_scale)
```

```python
import math

import jax
import jax.numpy as jnp
from jax import lax
from jax.sharding import PartitionSpec as P


def quick_gelu(values):
    return values * jax.nn.sigmoid(1.702 * values)


def gelu_slope(values):
    sigma = jax.nn.sigmoid(1.702 * values)
    return sigma + 1.702 * values * sigma * (1.0 - sigma)


def normalize(patch_rows, gain, shift):
    floats = patch_rows.astype(jnp.float32)
    row_mean = jnp.mean(floats, axis=-1, keepdims=True)
    centred = floats - row_mean
    row_var = jnp.mean(centred * centred, axis=-1, keepdims=True)
    scaled = centred * lax.rsqrt(row_var + 1e-06) * gain.astype(jnp.float32) + shift.astype(
        jnp.float32
    )
    return scaled.astype(jnp.bfloat16)


def local(
    patches,
    routes,
    gain,
    shift,
    first_weight,
    first_bias,
    adapter_down,
    adapter_up,
    second_weight,
    second_bias,
    language_slot_gradient,
):
    rank_count = lax.axis_size("dp")
    row_count = patches.shape[0]
    capacity = language_slot_gradient.shape[0] // rank_count
    destination = routes[:, 0]
    hit_table = (destination[:, None] == jnp.arange(rank_count, dtype=jnp.int32)[None, :]).astype(
        jnp.int32
    )
    before = jnp.cumsum(hit_table, axis=0) - hit_table
    rank_in = jnp.sum(before * hit_table, axis=1)
    slot_of = destination * capacity + rank_in
    placing = (
        slot_of[None, :] == jnp.arange(rank_count * capacity, dtype=jnp.int32)[:, None]
    ).astype(jnp.bfloat16)
    returned = lax.all_to_all(language_slot_gradient, "dp", split_axis=0, concat_axis=0, tiled=True)
    grad_local = lax.dot_general(
        placing, returned, (((0,), (0,)), ((), ())), preferred_element_type=jnp.float32
    ).astype(jnp.bfloat16)
    whole_rows = lax.all_gather(patches, "mp", axis=1, tiled=True)
    normalized_rows = normalize(whole_rows, gain, shift)
    adapter_latent = jnp.dot(
        normalized_rows, adapter_down, preferred_element_type=jnp.float32
    ).astype(jnp.bfloat16)
    first_full, second_full = (
        lax.all_gather(first_weight, "dp", axis=0, tiled=True),
        lax.all_gather(second_weight, "dp", axis=1, tiled=True),
    )
    pre_main = jnp.dot(normalized_rows, first_full, preferred_element_type=jnp.float32)
    preactivation = (
        pre_main
        + jnp.dot(adapter_latent, adapter_up, preferred_element_type=jnp.float32)
        + first_bias.astype(jnp.float32)
    )
    activated = quick_gelu(preactivation).astype(jnp.bfloat16)
    partial_out = jnp.dot(activated, second_full, preferred_element_type=jnp.float32)
    branch_out = lax.psum_scatter(
        partial_out.astype(jnp.bfloat16), "mp", scatter_dimension=1, tiled=True
    ).astype(jnp.float32)
    embeds = (patches.astype(jnp.float32) + branch_out + second_bias.astype(jnp.float32)).astype(
        jnp.bfloat16
    )
    outgoing = jnp.dot(placing, embeds, preferred_element_type=jnp.float32).astype(jnp.bfloat16)
    embeds_llm = lax.all_to_all(outgoing, "dp", split_axis=0, concat_axis=0, tiled=True)
    whole_grad = lax.all_gather(grad_local, "mp", axis=1, tiled=True)
    grad_act = lax.dot_general(
        whole_grad, second_full, (((1,), (1,)), ((), ())), preferred_element_type=jnp.float32
    )
    preactivation_gradient = (grad_act * gelu_slope(preactivation)).astype(jnp.bfloat16)
    adapter_gradient = lax.dot_general(
        preactivation_gradient,
        adapter_up,
        (((1,), (1,)), ((), ())),
        preferred_element_type=jnp.float32,
    )
    grad_b_part = lax.dot_general(
        adapter_latent,
        preactivation_gradient,
        (((0,), (0,)), ((), ())),
        preferred_element_type=jnp.float32,
    )
    grad_scale = 1.0 / math.sqrt(row_count * rank_count)
    adapter_gradient = jnp.sum(lax.all_gather(adapter_gradient, "mp", axis=0), axis=0)
    feature_count = patches.shape[1]
    own_normalized = lax.dynamic_slice_in_dim(
        normalized_rows, lax.axis_index("mp") * feature_count, feature_count, axis=1
    )
    grad_a_part = lax.dot_general(
        adapter_gradient,
        own_normalized.astype(jnp.float32),
        (((0,), (0,)), ((), ())),
        precision=lax.Precision.HIGHEST,
    )
    down_gradient, grad_b = sum_over_dp(grad_a_part, grad_b_part, rank_count, grad_scale)
    down_gradient = lax.all_gather(down_gradient, "mp", axis=1, tiled=True).T
    return (embeds_llm, down_gradient, grad_b)


def sum_over_dp(grad_a_part, grad_b_part, rank_count, grad_scale):
    lanes = 128
    shares, sizes = [], []
    for part in (grad_b_part, grad_a_part):
        share = part.reshape(rank_count, -1)
        sizes.append(share.shape[1])
        share = jnp.pad(share, ((0, 0), (0, -share.shape[1] % lanes)))
        shares.append(share.reshape(rank_count, -1, lanes))
    cut = shares[0].shape[1]
    sent = lax.all_to_all(
        jnp.concatenate(shares, axis=1), "dp", split_axis=0, concat_axis=0, tiled=True
    )
    own = jnp.sum(sent, axis=0) * grad_scale
    whole = lax.all_to_all(
        jnp.broadcast_to(own[None], (rank_count,) + own.shape),
        "dp",
        split_axis=0,
        concat_axis=0,
        tiled=True,
    )
    grad_b = whole[:, :cut].reshape(rank_count, -1)[:, : sizes[0]].reshape(grad_b_part.shape)
    grad_a = whole[:, cut:].reshape(rank_count, -1)[:, : sizes[1]].reshape(grad_a_part.shape)
    return grad_a, grad_b


def solution(mesh):
    placed = (
        P("dp", "mp"),
        P("dp", None),
        P(),
        P(),
        P("dp", "mp"),
        P("mp"),
        P(),
        P(None, "mp"),
        P("mp", "dp"),
        P("mp"),
        P("dp", "mp"),
    )
    return jax.shard_map(
        local,
        mesh=mesh,
        in_specs=placed,
        out_specs=(P("dp", "mp"), P(), P(None, "mp")),
        check_vma=False,
    )
```

```python
import math

import jax
import jax.numpy as jnp
from jax import lax
from jax.experimental import pallas as pl
from jax.experimental.pallas import tpu as pltpu

from jax.sharding import PartitionSpec as P

MESH = pl.DeviceIdType.MESH
X_CHIPS, Z_CHIPS = 4, 16
QUAD = 4
HALF = 8


def gather_kernel(
    pieces_ref, patches_ref, weights_ref, rows_ref,
    staged, quad_send, quad_recv, y_send, y_recv,
    ring_send, ring_recv, near_send, near_recv, far_send, far_recv,
    mate_send, mate_recv,
):
    dp, y = lax.axis_index("dp"), lax.axis_index("mp")
    core = lax.rem(dp, 2)
    z = lax.rem(dp // 2, Z_CHIPS)
    x = dp // (2 * Z_CHIPS)
    turn = 1 - 2 * core

    def dp_of(x_at, z_at, core_at):
        return (
            lax.rem(x_at + 2 * X_CHIPS, X_CHIPS) * Z_CHIPS + lax.rem(z_at + 2 * Z_CHIPS, Z_CHIPS)
        ) * 2 + core_at

    def block_at(x_at, z_at):
        z_in = lax.rem(z_at + 2 * Z_CHIPS, Z_CHIPS)
        x_in = lax.rem(x_at + 2 * X_CHIPS, X_CHIPS)
        return lax.rem(z_in, QUAD) * (X_CHIPS * QUAD) + x_in * QUAD + z_in // QUAD

    quad, lane = z // QUAD, lax.rem(z, QUAD)
    quad_peers = []
    for step in range(QUAD):
        for flip in range(2):
            if step or flip:
                other = lax.rem(lane + step, QUAD)
                quad_peers.append((other, dp_of(x, quad * QUAD + other, (core + flip) % 2)))
    ring_next = dp_of(x, z + turn, core)
    ring_last = dp_of(x, z - turn, core)
    x_next = dp_of(x + turn, z, core)
    x_last = dp_of(x - turn, z, core)
    mate = dp_of(x, z, 1 - core)

    barrier = pltpu.get_barrier_semaphore()
    greeted = [(peer, y) for _, peer in quad_peers]
    greeted += [(ring_next, y), (ring_last, y), (x_next, y), (x_last, y)]
    greeted += [(dp, lax.rem(y + step, 4)) for step in range(1, 4)]
    for peer in greeted:
        pl.semaphore_signal(barrier, inc=1, device_id=peer, device_id_type=MESH)
    pl.semaphore_wait(barrier, len(greeted))

    own = lane * 2 + core
    swaps = []
    for at, (other, peer) in enumerate(quad_peers):
        step, flip = (at + 1) // 2, (at + 1) % 2
        swaps.append(
            pltpu.make_async_remote_copy(
                src_ref=pieces_ref.at[other],
                dst_ref=staged.at[own],
                send_sem=quad_send.at[at],
                recv_sem=quad_recv.at[at],
                device_id=(peer, y),
                device_id_type=MESH,
            )
        )
        swaps[-1].start()
    rows_sent = []
    for step in range(1, 4):
        rows_sent.append(
            pltpu.make_async_remote_copy(
                src_ref=patches_ref,
                dst_ref=rows_ref.at[y],
                send_sem=y_send.at[step - 1],
                recv_sem=y_recv.at[step - 1],
                device_id=(dp, lax.rem(y + step, 4)),
                device_id_type=MESH,
            )
        )
        rows_sent[-1].start()
    staged[own] = pieces_ref[lane]
    rows_ref[y] = patches_ref[...]
    for swap in swaps:
        swap.wait_recv()
    into = lax.broadcasted_iota(jnp.int32, (80, 128), 0)
    out_of = lax.broadcasted_iota(jnp.int32, (80, 128), 1)
    merge = ((into // 10) * 16 + into % 10 == out_of).astype(jnp.bfloat16)
    mine = block_at(x, z)
    weights_ref[mine] = jnp.dot(
        merge, staged[...].reshape(128, 640), preferred_element_type=jnp.float32
    ).astype(jnp.bfloat16)

    def block_copy(block, sends, recvs, at, peer):
        return pltpu.make_async_remote_copy(
            src_ref=weights_ref.at[block],
            dst_ref=weights_ref.at[block],
            send_sem=sends.at[at],
            recv_sem=recvs.at[at],
            device_id=(peer, y),
            device_id_type=MESH,
        )

    sent = []

    def send(block, sends, recvs, at, peer):
        copy = block_copy(block, sends, recvs, at, peer)
        copy.start()
        sent.append(copy)

    def arrived(block, sends, recvs, at):
        block_copy(block, sends, recvs, at, mate).wait_recv()

    for step in range(HALF + 3):
        if step <= HALF:
            if step:
                arrived(block_at(x, z - turn * step), ring_send, ring_recv, step - 1)
            first = block_at(x, z - turn * step)
            if step < HALF:
                send(first, ring_send, ring_recv, step, ring_next)
            send(first, near_send, near_recv, 2 * step if step < HALF else 15, x_next)
            if 0 < step < HALF:
                send(first, mate_send, mate_recv, step, mate)
                second = block_at(x, z + turn * step)
                arrived(second, mate_send, mate_recv, step)
                send(second, near_send, near_recv, 2 * step - 1, x_next)
        before = step - 1
        if 0 <= before <= HALF:
            at = 2 * before if before < HALF else 15
            block = block_at(x - turn, z - turn * before)
            arrived(block, near_send, near_recv, at)
            if before == 0:
                @pl.when(core == 0)
                def _():
                    block_copy(block, far_send, far_recv, 0, x_next).start()
            elif before == HALF:
                @pl.when(core == 1)
                def _():
                    block_copy(block, far_send, far_recv, 0, x_next).start()
            else:
                send(block, far_send, far_recv, before, x_next)
            send(block, mate_send, mate_recv, 8 + at, mate)
            if 0 < before < HALF:
                block = block_at(x - turn, z + turn * before)
                arrived(block, near_send, near_recv, 2 * before - 1)
                send(block, mate_send, mate_recv, 8 + 2 * before - 1, mate)
        before = step - 2
        if 0 < before < HALF:
            block = block_at(x - 2 * turn, z - turn * before)
            arrived(block, far_send, far_recv, before)
            send(block, mate_send, mate_recv, 24 + before, mate)
    block = block_at(x - 2 * turn, z + HALF * core)
    arrived(block, far_send, far_recv, 0)
    send(block, mate_send, mate_recv, 24, mate)
    for at in range(16):
        arrived(mine, mate_send, mate_recv, 8 + at)
    for at in range(8):
        arrived(mine, mate_send, mate_recv, 24 + at)
    block_copy(mine, far_send, far_recv, 0, x_next).wait_send()
    for copy in sent + swaps:
        copy.wait_send()
    for copy in rows_sent:
        copy.wait()


def gather_all(first_weight, second_weight, patches):
    rows, columns = first_weight.shape
    stacked = jnp.stack([first_weight, second_weight.T])
    stacked = jnp.pad(stacked, ((0, 0), (0, 16 - rows), (0, 0)))
    pieces = stacked.reshape(2, 16, 2, columns // 2).transpose(0, 2, 1, 3).reshape(4, 16, 640)
    whole = pl.BlockSpec(memory_space=pltpu.VMEM)
    semaphores = [7, 7, 3, 3, 8, 8, 16, 16, 8, 8, 32, 32]
    weights, rows = pl.pallas_call(
        gather_kernel,
        out_shape=(
            jax.ShapeDtypeStruct((64, 80, 640), jnp.bfloat16),
            jax.ShapeDtypeStruct((4,) + patches.shape, jnp.bfloat16),
        ),
        in_specs=[whole, whole],
        out_specs=(whole, whole),
        scratch_shapes=[pltpu.VMEM((8, 16, 640), jnp.bfloat16)]
        + [pltpu.SemaphoreType.DMA((count,)) for count in semaphores],
        compiler_params=pltpu.CompilerParams(
            collective_id=0, has_side_effects=True, vmem_limit_bytes=32 * 1024 * 1024
        ),
        name="gather",
    )(pieces, patches)
    return weights.reshape(2, 2, 1280, 640), rows


def quick_gelu(values):
    return values * jax.nn.sigmoid(1.702 * values)


def gelu_slope(values):
    sigma = jax.nn.sigmoid(1.702 * values)
    return sigma + 1.702 * values * sigma * (1.0 - sigma)


def normalize(patch_rows, gain, shift):
    floats = patch_rows.astype(jnp.float32)
    row_mean = jnp.mean(floats, axis=-1, keepdims=True)
    centred = floats - row_mean
    row_var = jnp.mean(centred * centred, axis=-1, keepdims=True)
    scaled = centred * lax.rsqrt(row_var + 1e-06) * gain.astype(jnp.float32) + shift.astype(
        jnp.float32
    )
    return scaled.astype(jnp.bfloat16)


def local(
    patches,
    routes,
    gain,
    shift,
    first_weight,
    first_bias,
    adapter_down,
    adapter_up,
    second_weight,
    second_bias,
    language_slot_gradient,
):
    rank_count = lax.axis_size("dp")
    row_count = patches.shape[0]
    capacity = language_slot_gradient.shape[0] // rank_count
    destination = routes[:, 0]
    hit_table = (destination[:, None] == jnp.arange(rank_count, dtype=jnp.int32)[None, :]).astype(
        jnp.int32
    )
    before = jnp.cumsum(hit_table, axis=0) - hit_table
    rank_in = jnp.sum(before * hit_table, axis=1)
    slot_of = destination * capacity + rank_in
    placing = (
        slot_of[None, :] == jnp.arange(rank_count * capacity, dtype=jnp.int32)[:, None]
    ).astype(jnp.bfloat16)
    returned = lax.all_to_all(language_slot_gradient, "dp", split_axis=0, concat_axis=0, tiled=True)
    grad_local = lax.dot_general(
        placing, returned, (((0,), (0,)), ((), ())), preferred_element_type=jnp.float32
    ).astype(jnp.bfloat16)
    projections, rows_by_rank = gather_all(first_weight, second_weight, patches)
    whole_rows = jnp.concatenate(list(rows_by_rank), axis=1)
    normalized_rows = normalize(whole_rows, gain, shift)
    adapter_latent = jnp.dot(
        normalized_rows, adapter_down, preferred_element_type=jnp.float32
    ).astype(jnp.bfloat16)
    pre_main = jnp.concatenate(
        [
            jnp.dot(normalized_rows, half, preferred_element_type=jnp.float32)
            for half in projections[0]
        ],
        axis=1,
    )
    preactivation = (
        pre_main
        + jnp.dot(adapter_latent, adapter_up, preferred_element_type=jnp.float32)
        + first_bias.astype(jnp.float32)
    )
    activated = quick_gelu(preactivation).astype(jnp.bfloat16)
    hidden_halves = jnp.split(activated, 2, axis=1)
    partial_out = sum(
        lax.dot_general(
            part, half, (((1,), (1,)), ((), ())), preferred_element_type=jnp.float32
        )
        for part, half in zip(hidden_halves, projections[1])
    )
    branch_out = lax.psum_scatter(
        partial_out.astype(jnp.bfloat16), "mp", scatter_dimension=1, tiled=True
    ).astype(jnp.float32)
    embeds = (patches.astype(jnp.float32) + branch_out + second_bias.astype(jnp.float32)).astype(
        jnp.bfloat16
    )
    outgoing = jnp.dot(placing, embeds, preferred_element_type=jnp.float32).astype(jnp.bfloat16)
    embeds_llm = lax.all_to_all(outgoing, "dp", split_axis=0, concat_axis=0, tiled=True)
    whole_grad = lax.all_gather(grad_local, "mp", axis=1, tiled=True)
    grad_act = jnp.concatenate(
        [
            jnp.dot(whole_grad, half, preferred_element_type=jnp.float32)
            for half in projections[1]
        ],
        axis=1,
    )
    preactivation_gradient = (grad_act * gelu_slope(preactivation)).astype(jnp.bfloat16)
    adapter_gradient = lax.dot_general(
        preactivation_gradient,
        adapter_up,
        (((1,), (1,)), ((), ())),
        preferred_element_type=jnp.float32,
    )
    grad_b_part = lax.dot_general(
        adapter_latent,
        preactivation_gradient,
        (((0,), (0,)), ((), ())),
        preferred_element_type=jnp.float32,
    )
    grad_scale = 1.0 / math.sqrt(row_count * rank_count)
    adapter_gradient = jnp.sum(lax.all_gather(adapter_gradient, "mp", axis=0), axis=0)
    feature_count = patches.shape[1]
    own_normalized = lax.dynamic_slice_in_dim(
        normalized_rows, lax.axis_index("mp") * feature_count, feature_count, axis=1
    )
    grad_a_part = lax.dot_general(
        adapter_gradient,
        own_normalized.astype(jnp.float32),
        (((0,), (0,)), ((), ())),
        precision=lax.Precision.HIGHEST,
    )
    down_gradient, grad_b = sum_over_dp(grad_a_part, grad_b_part, rank_count, grad_scale)
    down_gradient = lax.all_gather(down_gradient, "mp", axis=1, tiled=True).T
    return (embeds_llm, down_gradient, grad_b)


def sum_over_dp(grad_a_part, grad_b_part, rank_count, grad_scale):
    lanes = 128
    shares, sizes = [], []
    for part in (grad_b_part, grad_a_part):
        share = part.reshape(rank_count, -1)
        sizes.append(share.shape[1])
        share = jnp.pad(share, ((0, 0), (0, -share.shape[1] % lanes)))
        shares.append(share.reshape(rank_count, -1, lanes))
    cut = shares[0].shape[1]
    sent = lax.all_to_all(
        jnp.concatenate(shares, axis=1), "dp", split_axis=0, concat_axis=0, tiled=True
    )
    own = jnp.sum(sent, axis=0) * grad_scale
    whole = lax.all_to_all(
        jnp.broadcast_to(own[None], (rank_count,) + own.shape),
        "dp",
        split_axis=0,
        concat_axis=0,
        tiled=True,
    )
    grad_b = whole[:, :cut].reshape(rank_count, -1)[:, : sizes[0]].reshape(grad_b_part.shape)
    grad_a = whole[:, cut:].reshape(rank_count, -1)[:, : sizes[1]].reshape(grad_a_part.shape)
    return grad_a, grad_b


def solution(mesh):
    placed = (
        P("dp", "mp"),
        P("dp", None),
        P(),
        P(),
        P("dp", "mp"),
        P("mp"),
        P(),
        P(None, "mp"),
        P("mp", "dp"),
        P("mp"),
        P("dp", "mp"),
    )
    return jax.shard_map(
        local,
        mesh=mesh,
        in_specs=placed,
        out_specs=(P("dp", "mp"), P(), P(None, "mp")),
        check_vma=False,
    )
```

```python
import math

import jax
import jax.numpy as jnp
from jax import lax
from jax.experimental import pallas as pl
from jax.experimental.pallas import tpu as pltpu
from jax.sharding import PartitionSpec as P

MESH = pl.DeviceIdType.MESH
X_CHIPS, Z_CHIPS, MP = 4, 16, 4
QUAD, HALF, OCT = 4, 8, 8
TILES, SUM_TILES = 16, 13
GRAD_B_TILES = 10


def one_hot(places, count):
    columns = lax.broadcasted_iota(jnp.int32, (places.shape[0], count), 1)
    return (columns == places).astype(jnp.bfloat16)


def f32_dot(a, b):
    return jnp.dot(a, b, preferred_element_type=jnp.float32)


def f32_dot_t(a, b):
    return lax.dot_general(a, b, (((1,), (1,)), ((), ())), preferred_element_type=jnp.float32)


def block_kernel(
    pieces_ref, patches_ref, slots_ref, place_row_ref, place_col_ref, gain_ref, shift_ref,
    first_bias_ref, down_ref, down_t_ref, up_ref, second_bias_ref,
    embeds_ref, grad_a_ref, grad_b_ref,
    weights, staged, rows, normed, grads, act, slope, partial, got_partial,
    in_a, in_b, in_c, in_e, out_a, out_b, out_c, out_e,
    lora, parts, got_parts, reduced, got_tiles, total, whole_b, rank_a, whole_a,
    quad_send, quad_recv, ring_send, ring_recv, near_send, near_recv, far_send, far_recv,
    mate_send, mate_recv, y_send, y_recv, z_send, z_recv, oct_send, oct_recv,
):
    dp, y = lax.axis_index("dp"), lax.axis_index("mp")
    core = lax.rem(dp, 2)
    z = lax.rem(dp // 2, Z_CHIPS)
    x = dp // (2 * Z_CHIPS)
    turn = 1 - 2 * core
    own_oct = x * 2 + core

    def dp_of(x_at, z_at, core_at):
        return (
            lax.rem(x_at + 2 * X_CHIPS, X_CHIPS) * Z_CHIPS + lax.rem(z_at + 2 * Z_CHIPS, Z_CHIPS)
        ) * 2 + core_at

    def block_at(x_at, z_at):
        z_in = lax.rem(z_at + 2 * Z_CHIPS, Z_CHIPS)
        x_in = lax.rem(x_at + 2 * X_CHIPS, X_CHIPS)
        return lax.rem(z_in, QUAD) * (X_CHIPS * QUAD) + x_in * QUAD + z_in // QUAD

    quad, lane = z // QUAD, lax.rem(z, QUAD)
    quad_peers = []
    for step in range(QUAD):
        for flip in range(2):
            if step or flip:
                other = lax.rem(lane + step, QUAD)
                quad_peers.append((other, dp_of(x, quad * QUAD + other, lax.rem(core + flip, 2))))
    ring_next = dp_of(x, z + turn, core)
    x_next = dp_of(x + turn, z, core)
    mate = dp_of(x, z, 1 - core)
    z_peers = [lax.rem(z + step, Z_CHIPS) for step in range(1, Z_CHIPS)]
    y_peers = [lax.rem(y + step, MP) for step in range(1, MP)]
    oct_peers = []
    for step in range(1, OCT):
        x_at, core_at = lax.rem(x + step // 2, X_CHIPS), lax.rem(core + step % 2, 2)
        oct_peers.append((x_at * 2 + core_at, dp_of(x_at, z, core_at)))

    barrier = pltpu.get_barrier_semaphore()
    greeted = [(peer, y) for _, peer in quad_peers]
    greeted += [(dp_of(x, z_at, core), y) for z_at in z_peers]
    greeted += [(peer, y) for _, peer in oct_peers]
    greeted += [(dp, y_at) for y_at in y_peers]
    for peer in greeted:
        pl.semaphore_signal(barrier, inc=1, device_id=peer, device_id_type=MESH)
    pl.semaphore_wait(barrier, len(greeted))

    sent = []

    def send(source, target, send_sem, recv_sem, peer, peer_y=None):
        copy = pltpu.make_async_remote_copy(
            src_ref=source,
            dst_ref=target,
            send_sem=send_sem,
            recv_sem=recv_sem,
            device_id=(peer, y if peer_y is None else peer_y),
            device_id_type=MESH,
        )
        copy.start()
        sent.append(copy)
        return copy

    def wait_all(copies):
        for copy in copies:
            copy.wait_recv()

    def to_y(buffer, phase):
        return [
            send(buffer.at[y], buffer.at[y], y_send.at[3 * phase + at], y_recv.at[3 * phase + at],
                 dp, y_at)
            for at, y_at in enumerate(y_peers)
        ]

    def to_z(source, target, phase):
        first = 15 * phase
        return [
            send(source.at[z_at], target.at[z], z_send.at[first + at], z_recv.at[first + at],
                 dp_of(x, z_at, core))
            for at, z_at in enumerate(z_peers)
        ]

    def to_oct(source_of, target, phase):
        first = 7 * phase
        return [
            send(source_of(at_oct), target, oct_send.at[first + at], oct_recv.at[first + at], peer)
            for at, (at_oct, peer) in enumerate(oct_peers)
        ]

    def block_copy(block, sends, recvs, at, peer):
        return pltpu.make_async_remote_copy(
            src_ref=weights.at[block],
            dst_ref=weights.at[block],
            send_sem=sends.at[at],
            recv_sem=recvs.at[at],
            device_id=(peer, y),
            device_id_type=MESH,
        )

    def send_block(block, sends, recvs, at, peer):
        copy = block_copy(block, sends, recvs, at, peer)
        copy.start()
        sent.append(copy)

    def arrived(block, sends, recvs, at):
        block_copy(block, sends, recvs, at, mate).wait_recv()

    def row_places(count):
        return lax.broadcasted_iota(jnp.int32, (count, 1), 0)

    def regroup_for_oct(received):
        n = row_places(512)
        place = (n // 4 % 16) * 32 + (n // 64) * 4 + n % 4
        return f32_dot(one_hot(place, 512), received[...].reshape(512, 320)).astype(
            jnp.bfloat16
        ).reshape(OCT, 64, 320)

    own = lane * 2 + core
    swaps = [
        send(pieces_ref.at[other], staged.at[own], quad_send.at[at], quad_recv.at[at], peer)
        for at, (other, peer) in enumerate(quad_peers)
    ]
    rows[y] = patches_ref[...]
    row_copies = to_y(rows, 0)
    staged[own] = pieces_ref[lane]

    n = row_places(512)
    place = (n // 8 % 4) * 128 + (n // 32) * 8 + n % 8
    in_a[...] = f32_dot(one_hot(place, 512), slots_ref[...]).astype(jnp.bfloat16).reshape(
        Z_CHIPS, 32, 320
    )
    in_b[z] = in_a[z]
    slot_copies = to_z(in_a, in_b, 0)

    wait_all(swaps)
    n = row_places(80)
    mine = block_at(x, z)
    weights[mine] = f32_dot(
        one_hot(n // 10 * 16 + n % 10, 128), staged[...].reshape(128, 640)
    ).astype(jnp.bfloat16)

    latents = []

    def norm_rows():
        wait_all(row_copies)
        floats = [rows[j].astype(jnp.float32) for j in range(MP)]
        mean = sum(jnp.sum(f, axis=-1, keepdims=True) for f in floats) * (1.0 / 1280)
        centred = [f - mean for f in floats]
        var = sum(jnp.sum(c * c, axis=-1, keepdims=True) for c in centred) * (1.0 / 1280)
        scale = lax.rsqrt(var + 1e-06)
        for j in range(MP):
            normed[j] = (centred[j] * scale * gain_ref[j] + shift_ref[j]).astype(jnp.bfloat16)
        latents.append(
            sum(f32_dot(normed[j], down_ref[j]) for j in range(MP)).astype(jnp.bfloat16)
        )
        latents.append(
            sum(f32_dot_t(down_t_ref[j], normed[j]) for j in range(MP)).astype(jnp.bfloat16)
        )

    slot_steps = []

    def slots_to_oct():
        wait_all(slot_copies)
        in_c[...] = regroup_for_oct(in_b)
        in_e[own_oct] = in_c[own_oct]
        slot_steps.append(to_oct(lambda o: in_c.at[o], in_e.at[own_oct], 0))

    def pick_grads():
        wait_all(slot_steps[0])
        grads[y] = f32_dot(
            one_hot(place_col_ref[...], 512), in_e[...].reshape(512, 320)
        ).astype(jnp.bfloat16)
        slot_steps.append(to_y(grads, 1))

    between = {2: norm_rows, 6: slots_to_oct, 9: pick_grads}

    for step in range(HALF + 3):
        if step <= HALF:
            if step:
                arrived(block_at(x, z - turn * step), ring_send, ring_recv, step - 1)
            first = block_at(x, z - turn * step)
            if step < HALF:
                send_block(first, ring_send, ring_recv, step, ring_next)
            send_block(first, near_send, near_recv, 2 * step if step < HALF else 15, x_next)
            if 0 < step < HALF:
                send_block(first, mate_send, mate_recv, step, mate)
                second = block_at(x, z + turn * step)
                arrived(second, mate_send, mate_recv, step)
                send_block(second, near_send, near_recv, 2 * step - 1, x_next)
        before = step - 1
        if 0 <= before <= HALF:
            at = 2 * before if before < HALF else 15
            block = block_at(x - turn, z - turn * before)
            arrived(block, near_send, near_recv, at)
            if before == 0:
                @pl.when(core == 0)
                def _():
                    block_copy(block, far_send, far_recv, 0, x_next).start()
            elif before == HALF:
                @pl.when(core == 1)
                def _():
                    block_copy(block, far_send, far_recv, 0, x_next).start()
            else:
                send_block(block, far_send, far_recv, before, x_next)
            send_block(block, mate_send, mate_recv, 8 + at, mate)
            if 0 < before < HALF:
                block = block_at(x - turn, z + turn * before)
                arrived(block, near_send, near_recv, 2 * before - 1)
                send_block(block, mate_send, mate_recv, 8 + 2 * before - 1, mate)
        before = step - 2
        if 0 < before < HALF:
            block = block_at(x - 2 * turn, z - turn * before)
            arrived(block, far_send, far_recv, before)
            send_block(block, mate_send, mate_recv, 24 + before, mate)
        if step in between:
            between[step]()
    block = block_at(x - 2 * turn, z + HALF * core)
    arrived(block, far_send, far_recv, 0)
    send_block(block, mate_send, mate_recv, 24, mate)
    for at in range(8, 32):
        arrived(mine, mate_send, mate_recv, at)

    latent, latent_t = latents

    def first_block(j, half):
        return weights[half * 16 + j * 4:half * 16 + j * 4 + 4].reshape(320, 640)

    def second_block(j, half):
        return weights[pl.ds((2 + half) * 16 + j * 4, 4)].reshape(320, 640)

    for half in range(2):
        pre = sum(f32_dot(normed[j], first_block(j, half)) for j in range(MP))
        pre = pre + f32_dot(latent, up_ref[half]) + first_bias_ref[half]
        sigma = jax.nn.sigmoid(1.702 * pre)
        act[half] = (pre * sigma).astype(jnp.bfloat16)
        slope[half] = sigma + 1.702 * pre * sigma * (1.0 - sigma)
    partial_copies = []
    for step in (1, 2, 3, 0):
        y_at = lax.rem(y + step, MP)
        partial[step] = sum(
            f32_dot_t(act[half], second_block(y_at, half)) for half in range(2)
        ).astype(jnp.bfloat16)
        if step:
            partial_copies.append(
                send(partial.at[step], got_partial.at[step - 1], y_send.at[5 + step],
                     y_recv.at[5 + step], dp, y_at)
            )

    wait_all(slot_steps[1])
    lora_t = jnp.zeros((64, 256), jnp.float32)
    for half in range(2):
        grad_act = sum(f32_dot(grads[j], second_block(j, half)) for j in range(MP))
        grad_pre = (grad_act * slope[half]).astype(jnp.bfloat16)
        lora_t = lora_t + f32_dot_t(up_ref[half], grad_pre)
        grad_b = f32_dot(latent_t, grad_pre)
        for o in range(OCT):
            for tile in range(5):
                parts[o, half * 5 + tile] = grad_b[8 * o:8 * o + 8, 128 * tile:128 * tile + 128]
    lora[y] = lora_t
    lora_copies = to_y(lora, 3)

    wait_all(partial_copies)
    branch = partial[0].astype(jnp.float32)
    for at in range(3):
        branch = branch + got_partial[at].astype(jnp.float32)
    embeds = (patches_ref[...].astype(jnp.float32) + branch + second_bias_ref[...]).astype(
        jnp.bfloat16
    )
    placing = (row_places(512) == place_row_ref[...]).astype(jnp.bfloat16)
    out_a[...] = f32_dot(placing, embeds).astype(jnp.bfloat16).reshape(Z_CHIPS, 32, 320)
    out_b[z] = out_a[z]
    out_copies = to_z(out_a, out_b, 1)

    wait_all(lora_copies)
    rest = lora[0] + lora[1] + lora[2] + lora[3]
    grad_a = jnp.zeros((64, 320), jnp.float32)
    own_normed = normed[y]
    for _ in range(3):
        top = rest.astype(jnp.bfloat16)
        rest = rest - top.astype(jnp.float32)
        grad_a = grad_a + f32_dot(top, own_normed)
    for o in range(OCT):
        strip = grad_a[8 * o:8 * o + 8]
        parts[o, 10] = strip[:, 0:128]
        parts[o, 11] = strip[:, 128:256]
        parts[o, 12] = jnp.concatenate([strip[:, 256:320], jnp.zeros((8, 64), jnp.float32)], 1)
    got_parts[own_oct] = parts[own_oct]
    part_copies = to_oct(lambda o: parts.at[o], got_parts.at[own_oct], 1)

    wait_all(part_copies)
    reduced[0:SUM_TILES] = jnp.sum(got_parts[...], axis=0)
    reduced[SUM_TILES:TILES] = jnp.zeros((TILES - SUM_TILES, 8, 128), jnp.float32)
    got_tiles[z] = reduced[z]
    tile_copies = to_z(reduced, got_tiles, 2)

    wait_all(out_copies)
    out_c[...] = regroup_for_oct(out_b)
    out_e[own_oct] = out_c[own_oct]
    oct_copies = to_oct(lambda o: out_c.at[o], out_e.at[own_oct], 2)

    wait_all(tile_copies)
    total[z] = jnp.sum(got_tiles[...], axis=0) * (1.0 / math.sqrt(32768))
    total_copies = [
        send(total.at[z], total.at[z], z_send.at[45 + at], z_recv.at[45 + at],
             dp_of(x, z_at, core))
        for at, z_at in enumerate(z_peers)
    ]

    wait_all(total_copies)
    rank_a[y] = total[GRAD_B_TILES:SUM_TILES]
    rank_copies = to_y(rank_a, 4)
    whole_b[own_oct] = total[0:GRAD_B_TILES]
    whole_b_copies = to_oct(lambda o: total.at[pl.ds(0, GRAD_B_TILES)], whole_b.at[own_oct], 3)
    wait_all(rank_copies)
    whole_a[own_oct] = rank_a[...]
    whole_a_copies = to_oct(lambda o: rank_a, whole_a.at[own_oct], 4)

    wait_all(oct_copies)
    n = row_places(512)
    place = (n // 128) * 128 + (n // 4 % 2) * 64 + (n // 8 % 16) * 4 + n % 4
    embeds_ref[...] = f32_dot(one_hot(place, 512), out_e[...].reshape(512, 320)).astype(
        jnp.bfloat16
    )
    wait_all(whole_b_copies)
    for o in range(OCT):
        for tile in range(GRAD_B_TILES):
            grad_b_ref[8 * o:8 * o + 8, 128 * tile:128 * tile + 128] = whole_b[o, tile]
    wait_all(whole_a_copies)
    for j in range(MP):
        for o in range(OCT):
            grad_a_ref[j, 8 * o:8 * o + 8, 0:128] = whole_a[o, j, 0]
            grad_a_ref[j, 8 * o:8 * o + 8, 128:256] = whole_a[o, j, 1]
            grad_a_ref[j, 8 * o:8 * o + 8, 256:320] = whole_a[o, j, 2][:, 0:64]

    block_copy(mine, far_send, far_recv, 0, x_next).wait_send()
    for copy in sent:
        copy.wait_send()


def local(
    patches,
    routes,
    gain,
    shift,
    first_weight,
    first_bias,
    adapter_down,
    adapter_up,
    second_weight,
    second_bias,
    language_slot_gradient,
):
    ranks = lax.axis_size("dp")
    bf16, f32 = jnp.bfloat16, jnp.float32
    destination = routes[:, 0]
    hits = (destination[:, None] == jnp.arange(ranks, dtype=jnp.int32)[None, :]).astype(jnp.int32)
    before = jnp.cumsum(hits, axis=0) - hits
    rank_in = jnp.sum(before * hits, axis=1)
    x_to, z_to, core_to = destination // 32, destination // 2 % 16, destination % 2
    place_out = z_to * 32 + x_to * 8 + core_to * 4 + rank_in
    place_in = x_to * 128 + core_to * 64 + z_to * 4 + rank_in

    rows, columns = first_weight.shape
    stacked = jnp.stack([first_weight, second_weight.T])
    stacked = jnp.pad(stacked, ((0, 0), (0, 16 - rows), (0, 0)))
    pieces = stacked.reshape(2, 16, 2, columns // 2).transpose(0, 2, 1, 3).reshape(4, 16, 640)
    down = adapter_down.reshape(4, 320, 64)

    whole = pl.BlockSpec(memory_space=pltpu.VMEM)
    semaphores = [7, 7, 8, 8, 16, 16, 8, 8, 32, 32, 15, 15, 60, 60, 35, 35]
    buffers = [
        ((64, 80, 640), bf16), ((8, 16, 640), bf16), ((4, 256, 320), bf16), ((4, 256, 320), bf16),
        ((4, 256, 320), bf16), ((2, 256, 640), bf16), ((2, 256, 640), f32), ((4, 256, 320), bf16),
        ((3, 256, 320), bf16),
        ((16, 32, 320), bf16), ((16, 32, 320), bf16), ((8, 64, 320), bf16), ((8, 64, 320), bf16),
        ((16, 32, 320), bf16), ((16, 32, 320), bf16), ((8, 64, 320), bf16), ((8, 64, 320), bf16),
        ((4, 64, 256), f32), ((8, 13, 8, 128), f32), ((8, 13, 8, 128), f32), ((16, 8, 128), f32),
        ((16, 8, 128), f32), ((16, 8, 128), f32), ((8, 10, 8, 128), f32), ((4, 3, 8, 128), f32),
        ((8, 4, 3, 8, 128), f32),
    ]
    embeds_llm, grad_a, grad_b = pl.pallas_call(
        block_kernel,
        out_shape=(
            jax.ShapeDtypeStruct((512, 320), bf16),
            jax.ShapeDtypeStruct((4, 64, 320), f32),
            jax.ShapeDtypeStruct((64, 1280), f32),
        ),
        in_specs=[whole] * 12,
        out_specs=(whole,) * 3,
        scratch_shapes=[pltpu.VMEM(shape, kind) for shape, kind in buffers]
        + [pltpu.SemaphoreType.DMA((count,)) for count in semaphores],
        compiler_params=pltpu.CompilerParams(
            collective_id=0, has_side_effects=True, vmem_limit_bytes=48 * 1024 * 1024
        ),
        name="block",
    )(
        pieces,
        patches,
        language_slot_gradient,
        place_out[None, :],
        place_in[:, None],
        gain.astype(f32).reshape(4, 1, 320),
        shift.astype(f32).reshape(4, 1, 320),
        first_bias.astype(f32).reshape(2, 1, 640),
        down,
        down.transpose(0, 2, 1),
        adapter_up.reshape(64, 2, 640).transpose(1, 0, 2),
        second_bias.astype(f32)[None, :],
    )
    return embeds_llm, grad_a.transpose(0, 2, 1).reshape(1280, 64), grad_b


def solution(mesh):
    placed = (
        P("dp", "mp"),
        P("dp", None),
        P(),
        P(),
        P("dp", "mp"),
        P("mp"),
        P(),
        P(None, "mp"),
        P("mp", "dp"),
        P("mp"),
        P("dp", "mp"),
    )
    return jax.shard_map(
        local,
        mesh=mesh,
        in_specs=placed,
        out_specs=(P("dp", "mp"), P(), P(None, "mp")),
        check_vma=False,
    )
```

```python
import math

import jax
import jax.numpy as jnp
from jax import lax
from jax.experimental import pallas as pl
from jax.experimental.pallas import tpu as pltpu
from jax.sharding import PartitionSpec as P

MESH = pl.DeviceIdType.MESH
X_CHIPS, Z_CHIPS, MP = 4, 16, 4
QUAD, HALF, OCT = 4, 8, 8
MATE_LAG, NEAR_LAG, FAR_LAG = 0, 1, 2
SLOT_STEPS = {HALF - 3: [1, 2, 3, 15, 14, 13], HALF - 2: [4, 5, 12, 11], HALF - 1: [6, 7, 10, 9, 8]}
TILES, SUM_TILES = 16, 13
GRAD_B_TILES, A_TILES = 10, 3


def one_hot(places, count):
    columns = lax.broadcasted_iota(jnp.int32, (places.shape[0], count), 1)
    return (columns == places).astype(jnp.bfloat16)


def f32_dot(a, b):
    return jnp.dot(a, b, preferred_element_type=jnp.float32)


def f32_dot_t(a, b):
    return lax.dot_general(a, b, (((1,), (1,)), ((), ())), preferred_element_type=jnp.float32)


def block_kernel(
    first_hbm, second_hbm, patches_hbm, slots_hbm, routes_hbm, gain_hbm, shift_hbm,
    first_bias_hbm, second_bias_hbm, down_hbm, up_hbm,
    embeds_ref, grad_a_ref, grad_b_ref,
    shards, patches_t, slots_t, routes_ref, gain_ref, shift_ref, first_bias_ref, second_bias_ref,
    down_ref, up_ref, pieces,
    weights, staged, rows, normed, grads, act, slope, partial, got_partial,
    in_a, in_b, in_c, in_e, out_a, out_b, out_c, out_e,
    parts_b, got_b, parts_a, got_a, reduced, got_tiles, total, whole_b, whole_a,
    quad_send, quad_recv, ring_send, ring_recv, near_send, near_recv, far_send, far_recv,
    mate_send, mate_recv, y_send, y_recv, z_send, z_recv, oct_send, oct_recv,
    wide_send, wide_recv, load_sem,
):
    dp, y = lax.axis_index("dp"), lax.axis_index("mp")
    core = lax.rem(dp, 2)
    z = lax.rem(dp // 2, Z_CHIPS)
    x = dp // (2 * Z_CHIPS)
    turn = 1 - 2 * core
    own_oct = x * 2 + core

    def dp_of(x_at, z_at, core_at):
        return x_at * (2 * Z_CHIPS) + z_at * 2 + core_at

    z_turned = {d: lax.rem(z + turn * d + Z_CHIPS, Z_CHIPS) for d in range(-HALF, HALF + 1)}
    x_turned = {d: lax.rem(x + turn * d + X_CHIPS, X_CHIPS) for d in range(-2, 2)}
    x_blocks = {d: x_turned[d] * Z_CHIPS for d in x_turned}

    def block_at(x_step, z_step):
        return x_blocks[x_step] + z_turned[z_step]

    def row_places(count):
        return lax.broadcasted_iota(jnp.int32, (count, 1), 0)

    other_core = 1 - core
    cores = (core, other_core)
    lane = lax.rem(z, QUAD)
    quad_peers = []
    for step in range(QUAD):
        other = lax.rem(lane + step, QUAD)
        for flip in range(2):
            if step or flip:
                quad_peers.append((other, dp_of(x, z - lane + other, cores[flip])))
    ring_next = dp_of(x, z_turned[1], core)
    x_next = dp_of(x_turned[1], z, core)
    mate = dp_of(x, z, other_core)
    z_peers = [lax.rem(z + step, Z_CHIPS) for step in range(1, Z_CHIPS)]
    z_peer_dps = [dp_of(x, z_at, core) for z_at in z_peers]
    y_peers = [lax.rem(y + step, MP) for step in range(1, MP)]
    oct_peers = []
    for step in range(1, OCT):
        x_at, core_at = lax.rem(x + step // 2, X_CHIPS), cores[step % 2]
        oct_peers.append((x_at * 2 + core_at, dp_of(x_at, z, core_at)))

    wide_peers = []
    for y_step in range(MP):
        y_at = y_peers[y_step - 1] if y_step else y
        if y_step:
            wide_peers.append((y_at, own_oct, dp))
        wide_peers += [(y_at, at_oct, peer) for at_oct, peer in oct_peers]

    loads = [
        pltpu.make_async_copy(source, target, load_sem.at[at])
        for at, (source, target) in enumerate((
            (first_hbm, shards.at[0]), (second_hbm, shards.at[1]), (patches_hbm, patches_t),
            (slots_hbm, slots_t), (routes_hbm, routes_ref), (gain_hbm, gain_ref), (shift_hbm, shift_ref),
            (first_bias_hbm, first_bias_ref), (second_bias_hbm, second_bias_ref),
            (down_hbm, down_ref),
            (up_hbm, up_ref),
        ))
    ]
    for load in loads:
        load.start()

    barrier = pltpu.get_barrier_semaphore()
    greeted = [(peer, y) for _, peer in quad_peers]
    greeted += [(peer, y) for peer in z_peer_dps]
    greeted += [(peer, y_at) for y_at, _, peer in wide_peers]
    for peer in greeted:
        pl.semaphore_signal(barrier, inc=1, device_id=peer, device_id_type=MESH)
    for load in loads[:4]:
        load.wait()
    for weight in range(2):
        for half in range(2):
            pieces[2 * weight + half, 0:10] = shards[weight, :, 640 * half:640 * half + 640]
            pieces[2 * weight + half, 10:16] = jnp.zeros((6, 640), jnp.bfloat16)
    own_rows = f32_dot_t(one_hot(row_places(256), 256), patches_t[...]).astype(jnp.bfloat16)
    rows[y] = own_rows
    pl.semaphore_wait(barrier, len(greeted))

    sent = []

    def send(source, target, send_sem, recv_sem, peer, peer_y=None):
        copy = pltpu.make_async_remote_copy(
            src_ref=source,
            dst_ref=target,
            send_sem=send_sem,
            recv_sem=recv_sem,
            device_id=(peer, y if peer_y is None else peer_y),
            device_id_type=MESH,
        )
        copy.start()
        sent.append(copy)
        return copy

    def wait_all(copies):
        for copy in copies:
            copy.wait_recv()

    def to_y(buffer, phase):
        return [
            send(buffer.at[y], buffer.at[y], y_send.at[3 * phase + at], y_recv.at[3 * phase + at],
                 dp, y_at)
            for at, y_at in enumerate(y_peers)
        ]

    def to_one_z(source, target, phase, offset):
        z_at, at = z_peers[offset - 1], 15 * phase + offset - 1
        return send(source.at[z_at], target.at[z], z_send.at[at], z_recv.at[at],
                    z_peer_dps[offset - 1])

    def to_z(source, target, phase):
        return [to_one_z(source, target, phase, offset) for offset in range(1, Z_CHIPS)]

    def to_oct(source_of, target, phase):
        first = 7 * phase
        return [
            send(source_of(at_oct), target, oct_send.at[first + at], oct_recv.at[first + at], peer)
            for at, (at_oct, peer) in enumerate(oct_peers)
        ]

    def to_wide(source_of, target, phase):
        first = 31 * phase
        return [
            send(source_of(y_at, at_oct), target, wide_send.at[first + at],
                 wide_recv.at[first + at], peer, y_at)
            for at, (y_at, at_oct, peer) in enumerate(wide_peers)
        ]

    def block_copy(block, sends, recvs, at, peer):
        return pltpu.make_async_remote_copy(
            src_ref=weights.at[block],
            dst_ref=weights.at[block],
            send_sem=sends.at[at],
            recv_sem=recvs.at[at],
            device_id=(peer, y),
            device_id_type=MESH,
        )

    def send_block(block, sends, recvs, at, peer):
        copy = block_copy(block, sends, recvs, at, peer)
        copy.start()
        sent.append(copy)

    def arrived(block, sends, recvs, at):
        block_copy(block, sends, recvs, at, mate).wait_recv()

    def regroup_for_oct(received):
        n = row_places(512)
        place = (n // 4 % 16) * 32 + (n // 64) * 4 + n % 4
        return f32_dot(one_hot(place, 512), received[...].reshape(512, 320)).astype(
            jnp.bfloat16
        ).reshape(OCT, 64, 320)

    own = lane * 2 + core
    swaps = [
        send(pieces.at[other], staged.at[own], quad_send.at[at], quad_recv.at[at], peer)
        for at, (other, peer) in enumerate(quad_peers)
    ]
    row_copies = to_y(rows, 0)
    staged[own] = pieces[lane]

    n = row_places(512)
    place = (n // 8 % 4) * 128 + (n // 32) * 8 + n % 8
    in_a[...] = f32_dot_t(one_hot(place, 512), slots_t[...]).astype(jnp.bfloat16).reshape(
        Z_CHIPS, 32, 320
    )
    in_b[z] = in_a[z]
    slot_copies = []

    wait_all(swaps)
    n = row_places(80)
    mine = block_at(0, 0)
    weights[mine] = f32_dot(
        one_hot(n // 10 * 16 + n % 10, 128), staged[...].reshape(128, 640)
    ).astype(jnp.bfloat16)

    latents, places = [], []

    def as_row(vector):
        return vector[...].astype(jnp.float32).reshape(1, vector.shape[0])

    def down_of(j):
        return down_ref[:, 320 * j:320 * j + 320]

    def up_of(half):
        return up_ref[:, 640 * half:640 * half + 640]

    def find_places():
        at_row = lax.broadcasted_iota(jnp.int32, (256, 256), 0)
        at_column = lax.broadcasted_iota(jnp.int32, (256, 256), 1)
        wide = jnp.where(at_row == at_column, routes_ref[...], 0).astype(jnp.float32)
        routes = jnp.sum(wide, axis=1, keepdims=True).astype(jnp.int32)
        hits = one_hot(routes, 128)
        before = f32_dot((at_column < at_row).astype(jnp.bfloat16), hits)
        rank_in = jnp.sum(before * hits.astype(jnp.float32), axis=1, keepdims=True)
        rank_in = rank_in.astype(jnp.int32)
        x_to, z_to, core_to = routes // 32, routes // 2 % 16, routes % 2
        place_out = z_to * 32 + x_to * 8 + core_to * 4 + rank_in
        wide = jnp.where(at_row == at_column, place_out, 0).astype(jnp.float32)
        places.append(jnp.sum(wide, axis=0, keepdims=True).astype(jnp.int32))
        places.append(x_to * 128 + core_to * 64 + z_to * 4 + rank_in)

    def norm_rows():
        for load in loads[4:]:
            load.wait()
        find_places()
        wait_all(row_copies)
        gain, shift = as_row(gain_ref), as_row(shift_ref)
        floats = [rows[j].astype(jnp.float32) for j in range(MP)]
        mean = sum(jnp.sum(f, axis=-1, keepdims=True) for f in floats) * (1.0 / 1280)
        centred = [f - mean for f in floats]
        var = sum(jnp.sum(c * c, axis=-1, keepdims=True) for c in centred) * (1.0 / 1280)
        scale = lax.rsqrt(var + 1e-06)
        for j in range(MP):
            features = slice(320 * j, 320 * j + 320)
            normed[j] = (centred[j] * scale * gain[:, features] + shift[:, features]).astype(
                jnp.bfloat16
            )
        latents.append(
            sum(f32_dot_t(normed[j], down_of(j)) for j in range(MP)).astype(jnp.bfloat16)
        )
        latents.append(
            sum(f32_dot_t(down_of(j), normed[j]) for j in range(MP)).astype(jnp.bfloat16)
        )

    slot_steps = []

    def slots_to_oct():
        wait_all(slot_copies)
        in_c[...] = regroup_for_oct(in_b)
        in_e[own_oct] = in_c[own_oct]
        slot_steps.append(to_oct(lambda o: in_c.at[o], in_e.at[own_oct], 0))

    def pick_grads():
        wait_all(slot_steps[0])
        grads[y] = f32_dot(
            one_hot(places[1], 512), in_e[...].reshape(512, 320)
        ).astype(jnp.bfloat16)
        slot_steps.append(to_y(grads, 1))

    between = {3: [norm_rows]}

    for step in range(HALF + 1 + FAR_LAG):
        if step <= HALF:
            first = block_at(0, -step)
            if step:
                arrived(first, ring_send, ring_recv, step - 1)
            if step < HALF:
                send_block(first, ring_send, ring_recv, step, ring_next)
            send_block(first, near_send, near_recv, 2 * step if step < HALF else 15, x_next)
            if 0 < step < HALF:
                send_block(first, mate_send, mate_recv, step, mate)
        if 0 < step - MATE_LAG < HALF:
            before = step - MATE_LAG
            second = block_at(0, before)
            arrived(second, mate_send, mate_recv, before)
            send_block(second, near_send, near_recv, 2 * before - 1, x_next)
        if step in SLOT_STEPS:
            for offset in SLOT_STEPS[step]:
                slot_copies.append(to_one_z(in_a, in_b, 0, offset))
        before = step - NEAR_LAG
        if 0 <= before <= HALF:
            at = 2 * before if before < HALF else 15
            block = block_at(-1, -before)
            arrived(block, near_send, near_recv, at)
            if before == 0:
                @pl.when(core == 0)
                def _():
                    block_copy(block, far_send, far_recv, 0, x_next).start()
            elif before == HALF:
                @pl.when(core == 1)
                def _():
                    block_copy(block, far_send, far_recv, 0, x_next).start()
            else:
                send_block(block, far_send, far_recv, before, x_next)
            send_block(block, mate_send, mate_recv, 8 + at, mate)
            if 0 < before < HALF:
                block = block_at(-1, before)
                arrived(block, near_send, near_recv, 2 * before - 1)
                send_block(block, mate_send, mate_recv, 8 + 2 * before - 1, mate)
        before = step - FAR_LAG
        if 0 < before < HALF:
            block = block_at(-2, -before)
            arrived(block, far_send, far_recv, before)
            send_block(block, mate_send, mate_recv, 24 + before, mate)
        for job in between.get(step, ()):
            job()
    block = x_blocks[-2] + lax.rem(z + HALF * core, Z_CHIPS)
    arrived(block, far_send, far_recv, 0)
    send_block(block, mate_send, mate_recv, 24, mate)
    for at in range(8, 32):
        arrived(mine, mate_send, mate_recv, at)

    latent, latent_t = latents
    first_bias = as_row(first_bias_ref)

    def first_block(j, half):
        return jnp.concatenate([weights[j * 16 + quad * 4 + half] for quad in range(4)], 0)

    def second_block(j, half):
        return jnp.concatenate([weights[j * 16 + quad * 4 + 2 + half] for quad in range(4)], 0)

    for half in range(2):
        pre = sum(f32_dot(normed[j], first_block(j, half)) for j in range(MP))
        pre = pre + f32_dot(latent, up_of(half)) + first_bias[:, 640 * half:640 * half + 640]
        sigma = jax.nn.sigmoid(1.702 * pre)
        act[half] = (pre * sigma).astype(jnp.bfloat16)
        slope[half] = sigma + 1.702 * pre * sigma * (1.0 - sigma)
    partial_copies = []
    for step in (1, 2, 3, 0):
        y_at = lax.rem(y + step, MP)
        partial[step] = sum(
            f32_dot_t(act[half], second_block(y_at, half)) for half in range(2)
        ).astype(jnp.bfloat16)
        if step:
            partial_copies.append(
                send(partial.at[step], got_partial.at[step - 1], y_send.at[5 + step],
                     y_recv.at[5 + step], dp, y_at)
            )

    slots_to_oct()
    pick_grads()

    wait_all(partial_copies)
    branch = partial[0].astype(jnp.float32)
    for at in range(3):
        branch = branch + got_partial[at].astype(jnp.float32)
    embeds = (
        rows[y].astype(jnp.float32) + branch + as_row(second_bias_ref)
    ).astype(jnp.bfloat16)
    placing = (row_places(512) == places[0]).astype(jnp.bfloat16)
    out_a[...] = f32_dot(placing, embeds).astype(jnp.bfloat16).reshape(Z_CHIPS, 32, 320)
    out_b[z] = out_a[z]
    out_copies = to_z(out_a, out_b, 1)

    wait_all(slot_steps[1])
    lora_t = jnp.zeros((64, 256), jnp.float32)
    for half in range(2):
        grad_act = sum(f32_dot(grads[j], second_block(j, half)) for j in range(MP))
        grad_pre = (grad_act * slope[half]).astype(jnp.bfloat16)
        lora_t = lora_t + f32_dot_t(up_of(half), grad_pre)
        grad_b = f32_dot(latent_t, grad_pre)
        for o in range(OCT):
            for tile in range(5):
                parts_b[o, half * 5 + tile] = grad_b[8 * o:8 * o + 8, 128 * tile:128 * tile + 128]
    got_b[own_oct] = parts_b[own_oct]
    b_copies = to_oct(lambda o: parts_b.at[o], got_b.at[own_oct], 1)

    tops = []
    for _ in range(3):
        tops.append(lora_t.astype(jnp.bfloat16))
        lora_t = lora_t - tops[-1].astype(jnp.float32)
    grad_a = jnp.concatenate(
        [sum(f32_dot(top, normed[j]) for top in tops) for j in range(MP)], axis=1
    )
    for tile in range(MP * A_TILES):
        for o in range(OCT):
            strip = (
                grad_a[8 * o:8 * o + 8, 128 * tile:128 * tile + 128]
                if tile < GRAD_B_TILES
                else jnp.zeros((8, 128), jnp.float32)
            )
            parts_a[tile // A_TILES, o, tile % A_TILES] = strip
    got_a[y, own_oct] = parts_a[y, own_oct]
    a_copies = to_wide(lambda y_at, o: parts_a.at[y_at, o], got_a.at[y, own_oct], 0)

    wait_all(b_copies)
    reduced[0:GRAD_B_TILES] = jnp.sum(got_b[...], axis=0)
    wait_all(a_copies)
    reduced[GRAD_B_TILES:SUM_TILES] = jnp.sum(got_a[...], axis=(0, 1))
    reduced[SUM_TILES:TILES] = jnp.zeros((TILES - SUM_TILES, 8, 128), jnp.float32)
    got_tiles[z] = reduced[z]
    tile_copies = to_z(reduced, got_tiles, 2)

    wait_all(out_copies)
    out_c[...] = regroup_for_oct(out_b)
    out_e[own_oct] = out_c[own_oct]
    oct_copies = to_oct(lambda o: out_c.at[o], out_e.at[own_oct], 2)

    wait_all(tile_copies)
    total[z] = jnp.sum(got_tiles[...], axis=0) * (1.0 / math.sqrt(32768))
    total_copies = [
        send(total.at[z], total.at[z], z_send.at[45 + at], z_recv.at[45 + at], peer)
        for at, peer in enumerate(z_peer_dps)
    ]

    wait_all(total_copies)
    whole_b[own_oct] = total[0:GRAD_B_TILES]
    whole_b_copies = to_oct(lambda o: total.at[pl.ds(0, GRAD_B_TILES)], whole_b.at[own_oct], 3)
    whole_a[y, own_oct] = total[GRAD_B_TILES:SUM_TILES]
    whole_a_copies = to_wide(
        lambda y_at, o: total.at[pl.ds(GRAD_B_TILES, A_TILES)], whole_a.at[y, own_oct], 1
    )

    wait_all(oct_copies)
    n = row_places(512)
    place = (n // 128) * 128 + (n // 4 % 2) * 64 + (n // 8 % 16) * 4 + n % 4
    embeds_ref[...] = f32_dot(one_hot(place, 512), out_e[...].reshape(512, 320)).astype(
        jnp.bfloat16
    )
    wait_all(whole_b_copies)
    for o in range(OCT):
        for tile in range(GRAD_B_TILES):
            grad_b_ref[8 * o:8 * o + 8, 128 * tile:128 * tile + 128] = whole_b[o, tile]
    wait_all(whole_a_copies)
    for tile in range(GRAD_B_TILES):
        for o in range(OCT):
            grad_a_ref[8 * o:8 * o + 8, 128 * tile:128 * tile + 128] = whole_a[
                tile // A_TILES, o, tile % A_TILES
            ]

    block_copy(mine, far_send, far_recv, 0, x_next).wait_send()
    for copy in sent:
        copy.wait_send()


def local(
    patches,
    routes,
    gain,
    shift,
    first_weight,
    first_bias,
    adapter_down,
    adapter_up,
    second_weight,
    second_bias,
    language_slot_gradient,
):
    bf16, f32 = jnp.bfloat16, jnp.float32
    whole = pl.BlockSpec(memory_space=pltpu.VMEM)
    semaphores = [7, 7, 8, 8, 16, 16, 8, 8, 32, 32, 9, 9, 60, 60, 28, 28, 62, 62, 11]
    buffers = [
        ((2, 10, 1280), bf16), ((320, 256), bf16), ((320, 512), bf16), ((1, 256), jnp.int32),
        ((1280,), bf16), ((1280,), bf16), ((1280,), bf16), ((320,), bf16),
        ((64, 1280), bf16), ((64, 1280), bf16),
        ((4, 16, 640), bf16),
        ((64, 80, 640), bf16), ((8, 16, 640), bf16), ((4, 256, 320), bf16), ((4, 256, 320), bf16),
        ((4, 256, 320), bf16), ((2, 256, 640), bf16), ((2, 256, 640), f32), ((4, 256, 320), bf16),
        ((3, 256, 320), bf16),
        ((16, 32, 320), bf16), ((16, 32, 320), bf16), ((8, 64, 320), bf16), ((8, 64, 320), bf16),
        ((16, 32, 320), bf16), ((16, 32, 320), bf16), ((8, 64, 320), bf16), ((8, 64, 320), bf16),
        ((8, 10, 8, 128), f32), ((8, 10, 8, 128), f32), ((4, 8, 3, 8, 128), f32),
        ((4, 8, 3, 8, 128), f32), ((16, 8, 128), f32), ((16, 8, 128), f32), ((16, 8, 128), f32),
        ((8, 10, 8, 128), f32), ((4, 8, 3, 8, 128), f32),
    ]
    embeds_llm, grad_a, grad_b = pl.pallas_call(
        block_kernel,
        out_shape=(
            jax.ShapeDtypeStruct((512, 320), bf16),
            jax.ShapeDtypeStruct((64, 1280), f32),
            jax.ShapeDtypeStruct((64, 1280), f32),
        ),
        in_specs=[pl.BlockSpec(memory_space=pl.ANY)] * 11,
        out_specs=(whole,) * 3,
        scratch_shapes=[pltpu.VMEM(shape, kind) for shape, kind in buffers]
        + [pltpu.SemaphoreType.DMA((count,)) for count in semaphores],
        compiler_params=pltpu.CompilerParams(
            collective_id=0, has_side_effects=True, vmem_limit_bytes=60 * 1024 * 1024
        ),
        name="block",
    )(
        first_weight,
        second_weight.T,
        patches.T,
        language_slot_gradient.T,
        routes.T,
        gain,
        shift,
        first_bias,
        second_bias,
        adapter_down.T,
        adapter_up,
    )
    return embeds_llm, grad_a.T, grad_b


def solution(mesh):
    placed = (
        P("dp", "mp"),
        P("dp", None),
        P(),
        P(),
        P("dp", "mp"),
        P("mp"),
        P(),
        P(None, "mp"),
        P("mp", "dp"),
        P("mp"),
        P("dp", "mp"),
    )
    return jax.shard_map(
        local,
        mesh=mesh,
        in_specs=placed,
        out_specs=(P("dp", "mp"), P(), P(None, "mp")),
        check_vma=False,
    )
```

```python
import math

import jax
import jax.numpy as jnp
from jax import lax
from jax.experimental import pallas as pl
from jax.experimental.pallas import tpu as pltpu
from jax.sharding import PartitionSpec as P

MESH = pl.DeviceIdType.MESH
X_CHIPS, Z_CHIPS, MP = 4, 16, 4
QUAD, HALF, OCT = 4, 8, 8
MATE_LAG, NEAR_LAG, FAR_LAG = 0, 1, 2
SLOT_STEPS = {HALF - 3: [1, 2, 3, 15, 14, 13], HALF - 2: [4, 5, 12, 11], HALF - 1: [6, 7, 10, 9, 8]}
TILES, SUM_TILES = 16, 13
GRAD_B_TILES, A_TILES = 10, 3


def one_hot(places, count):
    columns = lax.broadcasted_iota(jnp.int32, (places.shape[0], count), 1)
    return (columns == places).astype(jnp.bfloat16)


def f32_dot(a, b):
    return jnp.dot(a, b, preferred_element_type=jnp.float32)


def f32_dot_t(a, b):
    return lax.dot_general(a, b, (((1,), (1,)), ((), ())), preferred_element_type=jnp.float32)


def pack(values, groups):
    values = values.reshape(groups, -1, 320)
    half = values.shape[1] // 2
    tail = jnp.concatenate([values[:, :half, 256:320], values[:, half:, 256:320]], axis=2)
    return jnp.concatenate([values[:, :, 0:128], values[:, :, 128:256], tail], axis=1)


def unpack(packed):
    groups, count = packed.shape[0], packed.shape[1] * 2 // 5
    tail = packed[:, 2 * count:]
    tail = jnp.concatenate([tail[:, :, 0:64], tail[:, :, 64:128]], axis=1)
    return jnp.concatenate(
        [packed[:, :count], packed[:, count:2 * count], tail], axis=2
    ).reshape(groups * count, 320)


def block_kernel(
    first_hbm, second_hbm, patches_hbm, slots_hbm, routes_hbm, gain_hbm, shift_hbm,
    first_bias_hbm, second_bias_hbm, down_hbm, up_hbm,
    embeds_ref, grad_a_ref, grad_b_ref,
    shards, patches_t, slots_t, routes_ref, gain_ref, shift_ref, first_bias_ref, second_bias_ref,
    down_ref, up_ref, pieces,
    weights, staged, rows, normed, grads, act, slope, partial, got_partial,
    in_a, in_b, in_c, in_e, out_a, out_b, out_c, out_e,
    parts_b, got_b, parts_a, got_a, reduced, got_tiles, total, whole_b, whole_a,
    quad_send, quad_recv, ring_send, ring_recv, near_send, near_recv, far_send, far_recv,
    mate_send, mate_recv, y_send, y_recv, z_send, z_recv, oct_send, oct_recv,
    wide_send, wide_recv, load_sem,
):
    dp, y = lax.axis_index("dp"), lax.axis_index("mp")
    core = lax.rem(dp, 2)
    z = lax.rem(dp // 2, Z_CHIPS)
    x = dp // (2 * Z_CHIPS)
    turn = 1 - 2 * core
    own_oct = x * 2 + core

    def dp_of(x_at, z_at, core_at):
        return x_at * (2 * Z_CHIPS) + z_at * 2 + core_at

    z_turned = {d: lax.rem(z + turn * d + Z_CHIPS, Z_CHIPS) for d in range(-HALF, HALF + 1)}
    x_turned = {d: lax.rem(x + turn * d + X_CHIPS, X_CHIPS) for d in range(-2, 2)}
    x_blocks = {d: x_turned[d] * Z_CHIPS for d in x_turned}

    def block_at(x_step, z_step):
        return x_blocks[x_step] + z_turned[z_step]

    def row_places(count):
        return lax.broadcasted_iota(jnp.int32, (count, 1), 0)

    other_core = 1 - core
    cores = (core, other_core)
    lane = lax.rem(z, QUAD)
    quad_peers = []
    for step in range(QUAD):
        other = lax.rem(lane + step, QUAD)
        for flip in range(2):
            if step or flip:
                quad_peers.append((other, dp_of(x, z - lane + other, cores[flip])))
    ring_next = dp_of(x, z_turned[1], core)
    x_next = dp_of(x_turned[1], z, core)
    mate = dp_of(x, z, other_core)
    z_peers = [lax.rem(z + step, Z_CHIPS) for step in range(1, Z_CHIPS)]
    z_peer_dps = [dp_of(x, z_at, core) for z_at in z_peers]
    y_peers = [lax.rem(y + step, MP) for step in range(1, MP)]
    oct_peers = []
    for step in range(1, OCT):
        x_at, core_at = lax.rem(x + step // 2, X_CHIPS), cores[step % 2]
        oct_peers.append((x_at * 2 + core_at, dp_of(x_at, z, core_at)))

    wide_peers = []
    for y_step in range(MP):
        y_at = y_peers[y_step - 1] if y_step else y
        if y_step:
            wide_peers.append((y_at, own_oct, dp))
        wide_peers += [(y_at, at_oct, peer) for at_oct, peer in oct_peers]

    loads = [
        pltpu.make_async_copy(source, target, load_sem.at[at])
        for at, (source, target) in enumerate((
            (first_hbm, shards.at[0]), (second_hbm, shards.at[1]), (patches_hbm, patches_t),
            (slots_hbm, slots_t), (routes_hbm, routes_ref), (gain_hbm, gain_ref), (shift_hbm, shift_ref),
            (first_bias_hbm, first_bias_ref), (second_bias_hbm, second_bias_ref),
            (down_hbm, down_ref),
            (up_hbm, up_ref),
        ))
    ]
    for load in loads:
        load.start()

    barrier = pltpu.get_barrier_semaphore()
    greeted = [(peer, y) for _, peer in quad_peers]
    greeted += [(peer, y) for peer in z_peer_dps]
    greeted += [(peer, y_at) for y_at, _, peer in wide_peers]
    for peer in greeted:
        pl.semaphore_signal(barrier, inc=1, device_id=peer, device_id_type=MESH)
    for load in loads[:4]:
        load.wait()
    for weight in range(2):
        for half in range(2):
            pieces[2 * weight + half, 0:10] = shards[weight, :, 640 * half:640 * half + 640]
            pieces[2 * weight + half, 10:16] = jnp.zeros((6, 640), jnp.bfloat16)
    rows[y] = patches_t[...]
    pl.semaphore_wait(barrier, len(greeted))

    sent = []

    def send(source, target, send_sem, recv_sem, peer, peer_y=None):
        copy = pltpu.make_async_remote_copy(
            src_ref=source,
            dst_ref=target,
            send_sem=send_sem,
            recv_sem=recv_sem,
            device_id=(peer, y if peer_y is None else peer_y),
            device_id_type=MESH,
        )
        copy.start()
        sent.append(copy)
        return copy

    def wait_all(copies):
        for copy in copies:
            copy.wait_recv()

    def to_y(buffer, phase):
        return [
            send(buffer.at[y], buffer.at[y], y_send.at[3 * phase + at], y_recv.at[3 * phase + at],
                 dp, y_at)
            for at, y_at in enumerate(y_peers)
        ]

    def to_one_z(source, target, phase, offset):
        z_at, at = z_peers[offset - 1], 15 * phase + offset - 1
        return send(source.at[z_at], target.at[z], z_send.at[at], z_recv.at[at],
                    z_peer_dps[offset - 1])

    def to_z(source, target, phase):
        return [to_one_z(source, target, phase, offset) for offset in range(1, Z_CHIPS)]

    def to_oct(source_of, target, phase):
        first = 7 * phase
        return [
            send(source_of(at_oct), target, oct_send.at[first + at], oct_recv.at[first + at], peer)
            for at, (at_oct, peer) in enumerate(oct_peers)
        ]

    def to_wide(source_of, target, phase):
        first = 31 * phase
        return [
            send(source_of(y_at, at_oct), target, wide_send.at[first + at],
                 wide_recv.at[first + at], peer, y_at)
            for at, (y_at, at_oct, peer) in enumerate(wide_peers)
        ]

    def block_copy(block, sends, recvs, at, peer):
        return pltpu.make_async_remote_copy(
            src_ref=weights.at[block],
            dst_ref=weights.at[block],
            send_sem=sends.at[at],
            recv_sem=recvs.at[at],
            device_id=(peer, y),
            device_id_type=MESH,
        )

    def send_block(block, sends, recvs, at, peer):
        copy = block_copy(block, sends, recvs, at, peer)
        copy.start()
        sent.append(copy)

    def arrived(block, sends, recvs, at):
        block_copy(block, sends, recvs, at, mate).wait_recv()

    def regroup_for_oct(received):
        n = row_places(512)
        place = (n // 4 % 16) * 32 + (n // 64) * 4 + n % 4
        moved = f32_dot(one_hot(place, 512), unpack(received[...]))
        return pack(moved.astype(jnp.bfloat16), OCT)

    own = lane * 2 + core
    swaps = [
        send(pieces.at[other], staged.at[own], quad_send.at[at], quad_recv.at[at], peer)
        for at, (other, peer) in enumerate(quad_peers)
    ]
    row_copies = to_y(rows, 0)
    staged[own] = pieces[lane]

    n = row_places(512)
    place = (n // 8 % 4) * 128 + (n // 32) * 8 + n % 8
    moved = f32_dot_t(one_hot(place, 512), slots_t[...])
    in_a[...] = pack(moved.astype(jnp.bfloat16), Z_CHIPS)
    in_b[z] = in_a[z]
    slot_copies = []

    wait_all(swaps)
    n = row_places(80)
    mine = block_at(0, 0)
    weights[mine] = f32_dot(
        one_hot(n // 10 * 16 + n % 10, 128), staged[...].reshape(128, 640)
    ).astype(jnp.bfloat16)

    latents, places = [], []
    same = one_hot(row_places(256), 256)

    def as_row(vector):
        return vector[...].astype(jnp.float32).reshape(1, vector.shape[0])

    def down_of(j):
        return down_ref[:, 320 * j:320 * j + 320]

    def up_of(half):
        return up_ref[:, 640 * half:640 * half + 640]

    def find_places():
        at_row = lax.broadcasted_iota(jnp.int32, (256, 256), 0)
        at_column = lax.broadcasted_iota(jnp.int32, (256, 256), 1)
        wide = jnp.where(at_row == at_column, routes_ref[...], 0).astype(jnp.float32)
        routes = jnp.sum(wide, axis=1, keepdims=True).astype(jnp.int32)
        hits = one_hot(routes, 128)
        before = f32_dot((at_column < at_row).astype(jnp.bfloat16), hits)
        rank_in = jnp.sum(before * hits.astype(jnp.float32), axis=1, keepdims=True)
        rank_in = rank_in.astype(jnp.int32)
        x_to, z_to, core_to = routes // 32, routes // 2 % 16, routes % 2
        place_out = z_to * 32 + x_to * 8 + core_to * 4 + rank_in
        wide = jnp.where(at_row == at_column, place_out, 0).astype(jnp.float32)
        places.append(jnp.sum(wide, axis=0, keepdims=True).astype(jnp.int32))
        places.append(x_to * 128 + core_to * 64 + z_to * 4 + rank_in)

    def norm_rows():
        for load in loads[4:]:
            load.wait()
        find_places()
        wait_all(row_copies)
        gain, shift = as_row(gain_ref), as_row(shift_ref)
        floats = [f32_dot_t(same, rows[j]) for j in range(MP)]
        mean = sum(jnp.sum(f, axis=-1, keepdims=True) for f in floats) * (1.0 / 1280)
        centred = [f - mean for f in floats]
        var = sum(jnp.sum(c * c, axis=-1, keepdims=True) for c in centred) * (1.0 / 1280)
        scale = lax.rsqrt(var + 1e-06)
        for j in range(MP):
            features = slice(320 * j, 320 * j + 320)
            normed[j] = (centred[j] * scale * gain[:, features] + shift[:, features]).astype(
                jnp.bfloat16
            )
        latents.append(
            sum(f32_dot_t(normed[j], down_of(j)) for j in range(MP)).astype(jnp.bfloat16)
        )
        latents.append(
            sum(f32_dot_t(down_of(j), normed[j]) for j in range(MP)).astype(jnp.bfloat16)
        )

    slot_steps = []

    def slots_to_oct():
        wait_all(slot_copies)
        in_c[...] = regroup_for_oct(in_b)
        in_e[own_oct] = in_c[own_oct]
        slot_steps.append(to_oct(lambda o: in_c.at[o], in_e.at[own_oct], 0))

    def pick_grads():
        wait_all(slot_steps[0])
        picked = f32_dot(one_hot(places[1], 512), unpack(in_e[...])).astype(jnp.bfloat16)
        grads[y] = f32_dot_t(one_hot(row_places(320), 320), picked).astype(jnp.bfloat16)
        slot_steps.append(to_y(grads, 1))

    between = {3: [norm_rows]}

    for step in range(HALF + 1 + FAR_LAG):
        if step <= HALF:
            first = block_at(0, -step)
            if step:
                arrived(first, ring_send, ring_recv, step - 1)
            if step < HALF:
                send_block(first, ring_send, ring_recv, step, ring_next)
            send_block(first, near_send, near_recv, 2 * step if step < HALF else 15, x_next)
            if 0 < step < HALF:
                send_block(first, mate_send, mate_recv, step, mate)
        if 0 < step - MATE_LAG < HALF:
            before = step - MATE_LAG
            second = block_at(0, before)
            arrived(second, mate_send, mate_recv, before)
            send_block(second, near_send, near_recv, 2 * before - 1, x_next)
        if step in SLOT_STEPS:
            for offset in SLOT_STEPS[step]:
                slot_copies.append(to_one_z(in_a, in_b, 0, offset))
        before = step - NEAR_LAG
        if 0 <= before <= HALF:
            at = 2 * before if before < HALF else 15
            block = block_at(-1, -before)
            arrived(block, near_send, near_recv, at)
            if before == 0:
                @pl.when(core == 0)
                def _():
                    block_copy(block, far_send, far_recv, 0, x_next).start()
            elif before == HALF:
                @pl.when(core == 1)
                def _():
                    block_copy(block, far_send, far_recv, 0, x_next).start()
            else:
                send_block(block, far_send, far_recv, before, x_next)
            send_block(block, mate_send, mate_recv, 8 + at, mate)
            if 0 < before < HALF:
                block = block_at(-1, before)
                arrived(block, near_send, near_recv, 2 * before - 1)
                send_block(block, mate_send, mate_recv, 8 + 2 * before - 1, mate)
        before = step - FAR_LAG
        if 0 < before < HALF:
            block = block_at(-2, -before)
            arrived(block, far_send, far_recv, before)
            send_block(block, mate_send, mate_recv, 24 + before, mate)
        for job in between.get(step, ()):
            job()
    block = x_blocks[-2] + lax.rem(z + HALF * core, Z_CHIPS)
    arrived(block, far_send, far_recv, 0)
    send_block(block, mate_send, mate_recv, 24, mate)
    for at in range(8, 32):
        arrived(mine, mate_send, mate_recv, at)

    latent, latent_t = latents
    first_bias = as_row(first_bias_ref)

    def first_block(j, half):
        return jnp.concatenate([weights[j * 16 + quad * 4 + half] for quad in range(4)], 0)

    def second_block(j, half):
        return jnp.concatenate([weights[j * 16 + quad * 4 + 2 + half] for quad in range(4)], 0)

    for half in range(2):
        pre = sum(f32_dot(normed[j], first_block(j, half)) for j in range(MP))
        pre = pre + f32_dot(latent, up_of(half)) + first_bias[:, 640 * half:640 * half + 640]
        sigma = jax.nn.sigmoid(1.702 * pre)
        act[half] = (pre * sigma).astype(jnp.bfloat16)
        slope[half] = sigma + 1.702 * pre * sigma * (1.0 - sigma)
    partial_copies = []
    for step in (1, 2, 3, 0):
        y_at = lax.rem(y + step, MP)
        partial[step] = sum(
            f32_dot_t(second_block(y_at, half), act[half]) for half in range(2)
        ).astype(jnp.bfloat16)
        if step:
            partial_copies.append(
                send(partial.at[step], got_partial.at[step - 1], y_send.at[5 + step],
                     y_recv.at[5 + step], dp, y_at)
            )

    slots_to_oct()
    pick_grads()

    wait_all(partial_copies)
    branch = partial[0].astype(jnp.float32)
    for at in range(3):
        branch = branch + got_partial[at].astype(jnp.float32)
    at_row = lax.broadcasted_iota(jnp.int32, (320, 320), 0)
    at_column = lax.broadcasted_iota(jnp.int32, (320, 320), 1)
    bias = jnp.sum(
        jnp.where(at_row == at_column, as_row(second_bias_ref), 0.0), axis=1, keepdims=True
    )
    embeds = (patches_t[...].astype(jnp.float32) + branch + bias).astype(jnp.bfloat16)
    placing = (row_places(512) == places[0]).astype(jnp.bfloat16)
    out_a[...] = pack(f32_dot_t(placing, embeds).astype(jnp.bfloat16), Z_CHIPS)
    out_b[z] = out_a[z]
    out_copies = to_z(out_a, out_b, 1)

    wait_all(slot_steps[1])
    grad_rows = [f32_dot_t(same, grads[j]).astype(jnp.bfloat16) for j in range(MP)]
    lora_t = jnp.zeros((64, 256), jnp.float32)
    for half in range(2):
        grad_act = sum(f32_dot(grad_rows[j], second_block(j, half)) for j in range(MP))
        grad_pre = (grad_act * slope[half]).astype(jnp.bfloat16)
        lora_t = lora_t + f32_dot_t(up_of(half), grad_pre)
        grad_b = f32_dot(latent_t, grad_pre)
        for o in range(OCT):
            for tile in range(5):
                parts_b[o, half * 5 + tile] = grad_b[8 * o:8 * o + 8, 128 * tile:128 * tile + 128]
    got_b[own_oct] = parts_b[own_oct]
    b_copies = to_oct(lambda o: parts_b.at[o], got_b.at[own_oct], 1)

    tops = []
    for _ in range(3):
        tops.append(lora_t.astype(jnp.bfloat16))
        lora_t = lora_t - tops[-1].astype(jnp.float32)
    grad_a = jnp.concatenate(
        [sum(f32_dot(top, normed[j]) for top in tops) for j in range(MP)], axis=1
    )
    for tile in range(MP * A_TILES):
        for o in range(OCT):
            strip = (
                grad_a[8 * o:8 * o + 8, 128 * tile:128 * tile + 128]
                if tile < GRAD_B_TILES
                else jnp.zeros((8, 128), jnp.float32)
            )
            parts_a[tile // A_TILES, o, tile % A_TILES] = strip
    got_a[y, own_oct] = parts_a[y, own_oct]
    a_copies = to_wide(lambda y_at, o: parts_a.at[y_at, o], got_a.at[y, own_oct], 0)

    wait_all(b_copies)
    reduced[0:GRAD_B_TILES] = jnp.sum(got_b[...], axis=0)
    wait_all(a_copies)
    reduced[GRAD_B_TILES:SUM_TILES] = jnp.sum(got_a[...], axis=(0, 1))
    reduced[SUM_TILES:TILES] = jnp.zeros((TILES - SUM_TILES, 8, 128), jnp.float32)
    got_tiles[z] = reduced[z]
    tile_copies = to_z(reduced, got_tiles, 2)

    wait_all(out_copies)
    out_c[...] = regroup_for_oct(out_b)
    out_e[own_oct] = out_c[own_oct]
    oct_copies = to_oct(lambda o: out_c.at[o], out_e.at[own_oct], 2)

    wait_all(tile_copies)
    total[z] = jnp.sum(got_tiles[...], axis=0) * (1.0 / math.sqrt(32768))
    total_copies = [
        send(total.at[z], total.at[z], z_send.at[45 + at], z_recv.at[45 + at], peer)
        for at, peer in enumerate(z_peer_dps)
    ]

    wait_all(total_copies)
    whole_b[own_oct] = total[0:GRAD_B_TILES]
    whole_b_copies = to_oct(lambda o: total.at[pl.ds(0, GRAD_B_TILES)], whole_b.at[own_oct], 3)
    whole_a[y, own_oct] = total[GRAD_B_TILES:SUM_TILES]
    whole_a_copies = to_wide(
        lambda y_at, o: total.at[pl.ds(GRAD_B_TILES, A_TILES)], whole_a.at[y, own_oct], 1
    )

    wait_all(oct_copies)
    n = row_places(512)
    place = (n // 128) * 128 + (n // 4 % 2) * 64 + (n // 8 % 16) * 4 + n % 4
    embeds_ref[...] = f32_dot(one_hot(place, 512), unpack(out_e[...])).T.astype(jnp.bfloat16)
    wait_all(whole_b_copies)
    for o in range(OCT):
        for tile in range(GRAD_B_TILES):
            grad_b_ref[8 * o:8 * o + 8, 128 * tile:128 * tile + 128] = whole_b[o, tile]
    wait_all(whole_a_copies)
    for tile in range(GRAD_B_TILES):
        for o in range(OCT):
            grad_a_ref[8 * o:8 * o + 8, 128 * tile:128 * tile + 128] = whole_a[
                tile // A_TILES, o, tile % A_TILES
            ]

    block_copy(mine, far_send, far_recv, 0, x_next).wait_send()
    for copy in sent:
        copy.wait_send()


def local(
    patches,
    routes,
    gain,
    shift,
    first_weight,
    first_bias,
    adapter_down,
    adapter_up,
    second_weight,
    second_bias,
    language_slot_gradient,
):
    bf16, f32 = jnp.bfloat16, jnp.float32
    whole = pl.BlockSpec(memory_space=pltpu.VMEM)
    semaphores = [7, 7, 8, 8, 16, 16, 8, 8, 32, 32, 9, 9, 60, 60, 28, 28, 62, 62, 11]
    buffers = [
        ((2, 10, 1280), bf16), ((320, 256), bf16), ((320, 512), bf16), ((1, 256), jnp.int32),
        ((1280,), bf16), ((1280,), bf16), ((1280,), bf16), ((320,), bf16),
        ((64, 1280), bf16), ((64, 1280), bf16),
        ((4, 16, 640), bf16),
        ((64, 80, 640), bf16), ((8, 16, 640), bf16), ((4, 320, 256), bf16), ((4, 256, 320), bf16),
        ((4, 320, 256), bf16), ((2, 256, 640), bf16), ((2, 256, 640), f32), ((4, 320, 256), bf16),
        ((3, 320, 256), bf16),
        ((16, 80, 128), bf16), ((16, 80, 128), bf16), ((8, 160, 128), bf16), ((8, 160, 128), bf16),
        ((16, 80, 128), bf16), ((16, 80, 128), bf16), ((8, 160, 128), bf16), ((8, 160, 128), bf16),
        ((8, 10, 8, 128), f32), ((8, 10, 8, 128), f32), ((4, 8, 3, 8, 128), f32),
        ((4, 8, 3, 8, 128), f32), ((16, 8, 128), f32), ((16, 8, 128), f32), ((16, 8, 128), f32),
        ((8, 10, 8, 128), f32), ((4, 8, 3, 8, 128), f32),
    ]
    embeds_llm, grad_a, grad_b = pl.pallas_call(
        block_kernel,
        out_shape=(
            jax.ShapeDtypeStruct((320, 512), bf16),
            jax.ShapeDtypeStruct((64, 1280), f32),
            jax.ShapeDtypeStruct((64, 1280), f32),
        ),
        in_specs=[pl.BlockSpec(memory_space=pl.ANY)] * 11,
        out_specs=(whole,) * 3,
        scratch_shapes=[pltpu.VMEM(shape, kind) for shape, kind in buffers]
        + [pltpu.SemaphoreType.DMA((count,)) for count in semaphores],
        compiler_params=pltpu.CompilerParams(
            collective_id=0, has_side_effects=True, vmem_limit_bytes=60 * 1024 * 1024
        ),
        name="block",
    )(
        first_weight,
        second_weight.T,
        patches.T,
        language_slot_gradient.T,
        routes.T,
        gain,
        shift,
        first_bias,
        second_bias,
        adapter_down.T,
        adapter_up,
    )
    return embeds_llm.T, grad_a.T, grad_b


def solution(mesh):
    placed = (
        P("dp", "mp"),
        P("dp", None),
        P(),
        P(),
        P("dp", "mp"),
        P("mp"),
        P(),
        P(None, "mp"),
        P("mp", "dp"),
        P("mp"),
        P("dp", "mp"),
    )
    return jax.shard_map(
        local,
        mesh=mesh,
        in_specs=placed,
        out_specs=(P("dp", "mp"), P(), P(None, "mp")),
        check_vma=False,
    )
```

```python
import math

import jax
import jax.numpy as jnp
from jax import lax
from jax.experimental import pallas as pl
from jax.experimental.pallas import tpu as pltpu
from jax.sharding import PartitionSpec as P

MESH = pl.DeviceIdType.MESH
X_CHIPS, Z_CHIPS, MP = 4, 16, 4
QUAD, HALF, OCT = 4, 8, 8
MATE_LAG, NEAR_LAG, FAR_LAG = 0, 1, 2
SLOT_STEPS = {HALF - 3: [1, 2, 3, 15, 14, 13], HALF - 2: [4, 5, 12, 11], HALF - 1: [6, 7, 10, 9, 8]}
TILES, SUM_TILES = 16, 13
GRAD_B_TILES, A_TILES = 10, 3
FAR_FIRST = sorted(range(1, Z_CHIPS), key=lambda offset: abs(offset - HALF))


def one_hot(places, count):
    columns = lax.broadcasted_iota(jnp.int32, (places.shape[0], count), 1)
    return (columns == places).astype(jnp.bfloat16)


def f32_dot(a, b):
    return jnp.dot(a, b, preferred_element_type=jnp.float32)


def f32_dot_t(a, b):
    return lax.dot_general(a, b, (((1,), (1,)), ((), ())), preferred_element_type=jnp.float32)


def pack(values, groups):
    values = values.reshape(groups, -1, 320)
    half = values.shape[1] // 2
    tail = jnp.concatenate([values[:, :half, 256:320], values[:, half:, 256:320]], axis=2)
    return jnp.concatenate([values[:, :, 0:128], values[:, :, 128:256], tail], axis=1)


def unpack(packed):
    groups, count = packed.shape[0], packed.shape[1] * 2 // 5
    tail = packed[:, 2 * count:]
    tail = jnp.concatenate([tail[:, :, 0:64], tail[:, :, 64:128]], axis=1)
    return jnp.concatenate(
        [packed[:, :count], packed[:, count:2 * count], tail], axis=2
    ).reshape(groups * count, 320)


def block_kernel(
    first_hbm, second_hbm, patches_hbm, slots_hbm, routes_hbm, gain_hbm, shift_hbm,
    first_bias_hbm, second_bias_hbm, down_hbm, up_hbm,
    embeds_ref, grad_a_ref, grad_b_ref,
    shards, patches_t, slots_t, routes_ref, gain_ref, shift_ref, first_bias_ref, second_bias_ref,
    down_ref, up_ref, pieces,
    weights, staged, rows, normed, grads, act, slope, partial, got_partial,
    in_a, in_b, in_c, in_e, out_a, out_b, out_c, out_e,
    parts_b, got_b, parts_a, got_a, reduced, got_tiles, total, whole_b, whole_a,
    regroup, ordered, placing, picking, same_features,
    quad_send, quad_recv, ring_send, ring_recv, near_send, near_recv, far_send, far_recv,
    mate_send, mate_recv, y_send, y_recv, z_send, z_recv, oct_send, oct_recv,
    wide_send, wide_recv, end_send, end_recv, load_sem,
):
    dp, y = lax.axis_index("dp"), lax.axis_index("mp")
    core = lax.rem(dp, 2)
    z = lax.rem(dp // 2, Z_CHIPS)
    x = dp // (2 * Z_CHIPS)
    turn = 1 - 2 * core
    own_oct = x * 2 + core

    def dp_of(x_at, z_at, core_at):
        return x_at * (2 * Z_CHIPS) + z_at * 2 + core_at

    z_turned = {d: lax.rem(z + turn * d + Z_CHIPS, Z_CHIPS) for d in range(-HALF, HALF + 1)}
    x_turned = {d: lax.rem(x + turn * d + X_CHIPS, X_CHIPS) for d in range(-2, 2)}
    x_blocks = {d: x_turned[d] * Z_CHIPS for d in x_turned}

    def block_at(x_step, z_step):
        return x_blocks[x_step] + z_turned[z_step]

    def row_places(count):
        return lax.broadcasted_iota(jnp.int32, (count, 1), 0)

    other_core = 1 - core
    cores = (core, other_core)
    lane = lax.rem(z, QUAD)
    quad_peers = []
    for step in range(QUAD):
        other = lax.rem(lane + step, QUAD)
        for flip in range(2):
            if step or flip:
                quad_peers.append((other, dp_of(x, z - lane + other, cores[flip])))
    ring_next = dp_of(x, z_turned[1], core)
    x_next = dp_of(x_turned[1], z, core)
    mate = dp_of(x, z, other_core)
    z_peers = [lax.rem(z + step, Z_CHIPS) for step in range(1, Z_CHIPS)]
    z_peer_dps = [dp_of(x, z_at, core) for z_at in z_peers]
    y_peers = [lax.rem(y + step, MP) for step in range(1, MP)]
    oct_peers = []
    for step in range(1, OCT):
        x_at, core_at = lax.rem(x + step // 2, X_CHIPS), cores[step % 2]
        oct_peers.append((x_at * 2 + core_at, dp_of(x_at, z, core_at)))

    wide_peers = []
    for y_step in range(MP):
        y_at = y_peers[y_step - 1] if y_step else y
        if y_step:
            wide_peers.append((y_at, own_oct, dp))
        wide_peers += [(y_at, at_oct, peer) for at_oct, peer in oct_peers]

    x_peers = [lax.rem(x + step, X_CHIPS) for step in range(1, X_CHIPS)]
    x_peer_dps = [dp_of(x_at, z, core) for x_at in x_peers]
    plane_peers = [(y, peer) for peer in x_peer_dps]
    plane_peers += [(y_at, peer) for y_at in y_peers for peer in [dp] + x_peer_dps]

    loads = [
        pltpu.make_async_copy(source, target, load_sem.at[at])
        for at, (source, target) in enumerate((
            (first_hbm, shards.at[0]), (second_hbm, shards.at[1]), (patches_hbm, patches_t),
            (slots_hbm, slots_t), (routes_hbm, routes_ref), (gain_hbm, gain_ref), (shift_hbm, shift_ref),
            (first_bias_hbm, first_bias_ref), (second_bias_hbm, second_bias_ref),
            (down_hbm, down_ref),
            (up_hbm, up_ref),
        ))
    ]
    for load in loads:
        load.start()

    barrier = pltpu.get_barrier_semaphore()
    greeted = [(peer, y) for _, peer in quad_peers]
    greeted += [(peer, y) for peer in z_peer_dps]
    greeted += [(peer, y_at) for y_at, _, peer in wide_peers]
    for peer in greeted:
        pl.semaphore_signal(barrier, inc=1, device_id=peer, device_id_type=MESH)
    for load in loads[:4]:
        load.wait()
    for weight in range(2):
        for half in range(2):
            pieces[2 * weight + half, 0:10] = shards[weight, :, 640 * half:640 * half + 640]
            pieces[2 * weight + half, 10:16] = jnp.zeros((6, 640), jnp.bfloat16)
    rows[y] = patches_t[...]
    pl.semaphore_wait(barrier, len(greeted))

    sent = []

    def send(source, target, send_sem, recv_sem, peer, peer_y=None):
        copy = pltpu.make_async_remote_copy(
            src_ref=source,
            dst_ref=target,
            send_sem=send_sem,
            recv_sem=recv_sem,
            device_id=(peer, y if peer_y is None else peer_y),
            device_id_type=MESH,
        )
        copy.start()
        sent.append(copy)
        return copy

    def wait_all(copies):
        for copy in copies:
            copy.wait_recv()

    def to_y(buffer, phase):
        return [
            send(buffer.at[y], buffer.at[y], y_send.at[3 * phase + at], y_recv.at[3 * phase + at],
                 dp, y_at)
            for at, y_at in enumerate(y_peers)
        ]

    def to_one_z(source, target, phase, offset):
        z_at, at = z_peers[offset - 1], 15 * phase + offset - 1
        return send(source.at[z_at], target.at[z], z_send.at[at], z_recv.at[at],
                    z_peer_dps[offset - 1])

    def to_z(source, target, phase):
        return [to_one_z(source, target, phase, offset) for offset in FAR_FIRST]

    def to_oct(source_of, target, phase):
        first = 7 * phase
        return [
            send(source_of(at_oct), target, oct_send.at[first + at], oct_recv.at[first + at], peer)
            for at, (at_oct, peer) in enumerate(oct_peers)
        ]

    def to_wide(source_of, target, phase):
        first = 31 * phase
        return [
            send(source_of(y_at, at_oct), target, wide_send.at[first + at],
                 wide_recv.at[first + at], peer, y_at)
            for at, (y_at, at_oct, peer) in enumerate(wide_peers)
        ]

    def block_copy(block, sends, recvs, at, peer):
        return pltpu.make_async_remote_copy(
            src_ref=weights.at[block],
            dst_ref=weights.at[block],
            send_sem=sends.at[at],
            recv_sem=recvs.at[at],
            device_id=(peer, y),
            device_id_type=MESH,
        )

    def send_block(block, sends, recvs, at, peer):
        copy = block_copy(block, sends, recvs, at, peer)
        copy.start()
        sent.append(copy)

    def arrived(block, sends, recvs, at):
        block_copy(block, sends, recvs, at, mate).wait_recv()

    def regroup_for_oct(received):
        moved = f32_dot(regroup[...], unpack(received[...]))
        return pack(moved.astype(jnp.bfloat16), OCT)

    own = lane * 2 + core
    swaps = [
        send(pieces.at[other], staged.at[own], quad_send.at[at], quad_recv.at[at], peer)
        for at, (other, peer) in enumerate(quad_peers)
    ]
    row_copies = to_y(rows, 0)
    staged[own] = pieces[lane]

    n = row_places(512)
    place = (n // 8 % 4) * 128 + (n // 32) * 8 + n % 8
    moved = f32_dot_t(one_hot(place, 512), slots_t[...])
    in_a[...] = pack(moved.astype(jnp.bfloat16), Z_CHIPS)
    in_b[z] = in_a[z]
    slot_copies = []

    wait_all(swaps)
    n = row_places(80)
    mine = block_at(0, 0)
    weights[mine] = f32_dot(
        one_hot(n // 10 * 16 + n % 10, 128), staged[...].reshape(128, 640)
    ).astype(jnp.bfloat16)

    latents, places = [], []
    same = one_hot(row_places(256), 256)

    def as_row(vector):
        return vector[...].astype(jnp.float32).reshape(1, vector.shape[0])

    def down_of(j):
        return down_ref[:, 320 * j:320 * j + 320]

    def up_of(half):
        return up_ref[:, 640 * half:640 * half + 640]

    def find_places():
        at_row = lax.broadcasted_iota(jnp.int32, (256, 256), 0)
        at_column = lax.broadcasted_iota(jnp.int32, (256, 256), 1)
        wide = jnp.where(at_row == at_column, routes_ref[...], 0).astype(jnp.float32)
        routes = jnp.sum(wide, axis=1, keepdims=True).astype(jnp.int32)
        hits = one_hot(routes, 128)
        before = f32_dot((at_column < at_row).astype(jnp.bfloat16), hits)
        rank_in = jnp.sum(before * hits.astype(jnp.float32), axis=1, keepdims=True)
        rank_in = rank_in.astype(jnp.int32)
        x_to, z_to, core_to = routes // 32, routes // 2 % 16, routes % 2
        place_out = z_to * 32 + x_to * 8 + core_to * 4 + rank_in
        wide = jnp.where(at_row == at_column, place_out, 0).astype(jnp.float32)
        places.append(jnp.sum(wide, axis=0, keepdims=True).astype(jnp.int32))
        places.append(x_to * 128 + core_to * 64 + z_to * 4 + rank_in)

    def norm_rows():
        for load in loads[4:]:
            load.wait()
        find_places()
        wait_all(row_copies)
        gain, shift = as_row(gain_ref), as_row(shift_ref)
        floats = [f32_dot_t(same, rows[j]) for j in range(MP)]
        mean = sum(jnp.sum(f, axis=-1, keepdims=True) for f in floats) * (1.0 / 1280)
        centred = [f - mean for f in floats]
        var = sum(jnp.sum(c * c, axis=-1, keepdims=True) for c in centred) * (1.0 / 1280)
        scale = lax.rsqrt(var + 1e-06)
        for j in range(MP):
            features = slice(320 * j, 320 * j + 320)
            normed[j] = (centred[j] * scale * gain[:, features] + shift[:, features]).astype(
                jnp.bfloat16
            )
        latents.append(
            sum(f32_dot_t(normed[j], down_of(j)) for j in range(MP)).astype(jnp.bfloat16)
        )
        latents.append(
            sum(f32_dot_t(down_of(j), normed[j]) for j in range(MP)).astype(jnp.bfloat16)
        )

    slot_steps = []

    def make_moves():
        n = row_places(512)
        regroup[...] = one_hot((n // 4 % 16) * 32 + (n // 64) * 4 + n % 4, 512)
        ordered[...] = one_hot(
            (n // 128) * 128 + (n // 4 % 2) * 64 + (n // 8 % 16) * 4 + n % 4, 512
        )
        placing[...] = (n == places[0]).astype(jnp.bfloat16)
        picking[...] = one_hot(places[1], 512)
        same_features[...] = one_hot(row_places(320), 320)

    def slots_to_oct():
        wait_all(slot_copies)
        in_c[...] = regroup_for_oct(in_b)
        in_e[own_oct] = in_c[own_oct]
        slot_steps.append(to_oct(lambda o: in_c.at[o], in_e.at[own_oct], 0))

    def pick_grads():
        wait_all(slot_steps[0])
        picked = f32_dot(picking[...], unpack(in_e[...])).astype(jnp.bfloat16)
        grads[y] = f32_dot_t(same_features[...], picked).astype(jnp.bfloat16)
        slot_steps.append(to_y(grads, 1))

    between = {3: [norm_rows], 6: [make_moves]}

    for step in range(HALF + 1 + FAR_LAG):
        if step <= HALF:
            first = block_at(0, -step)
            if step:
                arrived(first, ring_send, ring_recv, step - 1)
            if step < HALF:
                send_block(first, ring_send, ring_recv, step, ring_next)
            send_block(first, near_send, near_recv, 2 * step if step < HALF else 15, x_next)
            if 0 < step < HALF:
                send_block(first, mate_send, mate_recv, step, mate)
        if 0 < step - MATE_LAG < HALF:
            before = step - MATE_LAG
            second = block_at(0, before)
            arrived(second, mate_send, mate_recv, before)
            send_block(second, near_send, near_recv, 2 * before - 1, x_next)
        if step in SLOT_STEPS:
            for offset in SLOT_STEPS[step]:
                slot_copies.append(to_one_z(in_a, in_b, 0, offset))
        before = step - NEAR_LAG
        if 0 <= before <= HALF:
            at = 2 * before if before < HALF else 15
            block = block_at(-1, -before)
            arrived(block, near_send, near_recv, at)
            if before == 0:
                @pl.when(core == 0)
                def _():
                    block_copy(block, far_send, far_recv, 0, x_next).start()
            elif before == HALF:
                @pl.when(core == 1)
                def _():
                    block_copy(block, far_send, far_recv, 0, x_next).start()
            else:
                send_block(block, far_send, far_recv, before, x_next)
            send_block(block, mate_send, mate_recv, 8 + at, mate)
            if 0 < before < HALF:
                block = block_at(-1, before)
                arrived(block, near_send, near_recv, 2 * before - 1)
                send_block(block, mate_send, mate_recv, 8 + 2 * before - 1, mate)
        before = step - FAR_LAG
        if 0 < before < HALF:
            block = block_at(-2, -before)
            arrived(block, far_send, far_recv, before)
            send_block(block, mate_send, mate_recv, 24 + before, mate)
        for job in between.get(step, ()):
            job()
    block = x_blocks[-2] + lax.rem(z + HALF * core, Z_CHIPS)
    arrived(block, far_send, far_recv, 0)
    send_block(block, mate_send, mate_recv, 24, mate)
    for at in range(8, 32):
        arrived(mine, mate_send, mate_recv, at)

    latent, latent_t = latents
    first_bias = as_row(first_bias_ref)

    def first_block(j, half):
        return jnp.concatenate([weights[j * 16 + quad * 4 + half] for quad in range(4)], 0)

    def second_block(j, half):
        return jnp.concatenate([weights[j * 16 + quad * 4 + 2 + half] for quad in range(4)], 0)

    for half in range(2):
        pre = sum(f32_dot(normed[j], first_block(j, half)) for j in range(MP))
        pre = pre + f32_dot(latent, up_of(half)) + first_bias[:, 640 * half:640 * half + 640]
        sigma = jax.nn.sigmoid(1.702 * pre)
        act[half] = (pre * sigma).astype(jnp.bfloat16)
        slope[half] = sigma + 1.702 * pre * sigma * (1.0 - sigma)
    partial_copies = []
    for step in (2, 1, 3, 0):
        y_at = lax.rem(y + step, MP)
        partial[step] = sum(
            f32_dot_t(second_block(y_at, half), act[half]) for half in range(2)
        ).astype(jnp.bfloat16)
        if step:
            partial_copies.append(
                send(partial.at[step], got_partial.at[step - 1], y_send.at[5 + step],
                     y_recv.at[5 + step], dp, y_at)
            )

    slots_to_oct()
    pick_grads()

    wait_all(partial_copies)
    branch = partial[0].astype(jnp.float32)
    for at in range(3):
        branch = branch + got_partial[at].astype(jnp.float32)
    at_row = lax.broadcasted_iota(jnp.int32, (320, 320), 0)
    at_column = lax.broadcasted_iota(jnp.int32, (320, 320), 1)
    bias = jnp.sum(
        jnp.where(at_row == at_column, as_row(second_bias_ref), 0.0), axis=1, keepdims=True
    )
    embeds = (patches_t[...].astype(jnp.float32) + branch + bias).astype(jnp.bfloat16)
    out_a[...] = pack(f32_dot_t(placing[...], embeds).astype(jnp.bfloat16), Z_CHIPS)
    out_b[z] = out_a[z]
    out_copies = to_z(out_a, out_b, 1)

    wait_all(slot_steps[1])
    grad_rows = [f32_dot_t(same, grads[j]).astype(jnp.bfloat16) for j in range(MP)]
    lora_t = jnp.zeros((64, 256), jnp.float32)
    for half in range(2):
        grad_act = sum(f32_dot(grad_rows[j], second_block(j, half)) for j in range(MP))
        grad_pre = (grad_act * slope[half]).astype(jnp.bfloat16)
        lora_t = lora_t + f32_dot_t(up_of(half), grad_pre)
        grad_b = f32_dot(latent_t, grad_pre)
        for o in range(OCT):
            for tile in range(5):
                parts_b[o, half * 5 + tile] = grad_b[8 * o:8 * o + 8, 128 * tile:128 * tile + 128]
    got_b[own_oct] = parts_b[own_oct]
    b_copies = to_oct(lambda o: parts_b.at[o], got_b.at[own_oct], 1)

    tops = []
    for _ in range(3):
        tops.append(lora_t.astype(jnp.bfloat16))
        lora_t = lora_t - tops[-1].astype(jnp.float32)
    grad_a = jnp.concatenate(
        [sum(f32_dot(top, normed[j]) for top in tops) for j in range(MP)], axis=1
    )
    for tile in range(MP * A_TILES):
        for o in range(OCT):
            strip = (
                grad_a[8 * o:8 * o + 8, 128 * tile:128 * tile + 128]
                if tile < GRAD_B_TILES
                else jnp.zeros((8, 128), jnp.float32)
            )
            parts_a[tile // A_TILES, o, tile % A_TILES] = strip
    got_a[y, own_oct] = parts_a[y, own_oct]
    a_copies = to_wide(lambda y_at, o: parts_a.at[y_at, o], got_a.at[y, own_oct], 0)

    wait_all(b_copies)
    reduced[0:GRAD_B_TILES] = jnp.sum(got_b[...], axis=0)
    wait_all(a_copies)
    reduced[GRAD_B_TILES:SUM_TILES] = jnp.sum(got_a[...], axis=(0, 1))
    reduced[SUM_TILES:TILES] = jnp.zeros((TILES - SUM_TILES, 8, 128), jnp.float32)
    got_tiles[z] = reduced[z]
    tile_copies = to_z(reduced, got_tiles, 2)

    wait_all(out_copies)
    out_c[...] = regroup_for_oct(out_b)
    out_e[own_oct] = out_c[own_oct]
    oct_copies = to_oct(lambda o: out_c.at[o], out_e.at[own_oct], 2)

    wait_all(tile_copies)
    total[z] = jnp.sum(got_tiles[...], axis=0) * (1.0 / math.sqrt(32768))
    total_copies = [
        send(total.at[z], total.at[z], z_send.at[45 + at], z_recv.at[45 + at], peer)
        for at, peer in ((offset - 1, z_peer_dps[offset - 1]) for offset in FAR_FIRST)
    ]

    wait_all(total_copies)
    whole_b[core, x] = total[0:GRAD_B_TILES]
    whole_a[core, y, x] = total[GRAD_B_TILES:SUM_TILES]
    b_target, a_target = whole_b.at[core, x], whole_a.at[core, y, x]
    whole_copies = [
        send(total.at[pl.ds(0, GRAD_B_TILES)], b_target, end_send.at[at], end_recv.at[at], peer)
        for at, peer in enumerate(x_peer_dps)
    ]
    whole_copies += [
        send(total.at[pl.ds(GRAD_B_TILES, A_TILES)], a_target, end_send.at[3 + at],
             end_recv.at[3 + at], peer, y_at)
        for at, (y_at, peer) in enumerate(plane_peers)
    ]

    wait_all(whole_copies)
    mate_copies = [
        send(whole.at[core], whole.at[core], end_send.at[18 + at], end_recv.at[18 + at], mate)
        for at, whole in enumerate((whole_b, whole_a))
    ]
    wait_all(oct_copies)
    embeds_ref[...] = f32_dot(ordered[...], unpack(out_e[...])).T.astype(jnp.bfloat16)
    wait_all(mate_copies)
    for o in range(OCT):
        for tile in range(GRAD_B_TILES):
            grad_b_ref[8 * o:8 * o + 8, 128 * tile:128 * tile + 128] = whole_b[
                o % 2, o // 2, tile
            ]
    for tile in range(GRAD_B_TILES):
        for o in range(OCT):
            grad_a_ref[8 * o:8 * o + 8, 128 * tile:128 * tile + 128] = whole_a[
                o % 2, tile // A_TILES, o // 2, tile % A_TILES
            ]

    block_copy(mine, far_send, far_recv, 0, x_next).wait_send()
    for copy in sent:
        copy.wait_send()


def local(
    patches,
    routes,
    gain,
    shift,
    first_weight,
    first_bias,
    adapter_down,
    adapter_up,
    second_weight,
    second_bias,
    language_slot_gradient,
):
    bf16, f32 = jnp.bfloat16, jnp.float32
    whole = pl.BlockSpec(memory_space=pltpu.VMEM)
    semaphores = [7, 7, 8, 8, 16, 16, 8, 8, 32, 32, 9, 9, 60, 60, 21, 21, 31, 31, 20, 20, 11]
    buffers = [
        ((2, 10, 1280), bf16), ((320, 256), bf16), ((320, 512), bf16), ((1, 256), jnp.int32),
        ((1280,), bf16), ((1280,), bf16), ((1280,), bf16), ((320,), bf16),
        ((64, 1280), bf16), ((64, 1280), bf16),
        ((4, 16, 640), bf16),
        ((64, 80, 640), bf16), ((8, 16, 640), bf16), ((4, 320, 256), bf16), ((4, 256, 320), bf16),
        ((4, 320, 256), bf16), ((2, 256, 640), bf16), ((2, 256, 640), f32), ((4, 320, 256), bf16),
        ((3, 320, 256), bf16),
        ((16, 80, 128), bf16), ((16, 80, 128), bf16), ((8, 160, 128), bf16), ((8, 160, 128), bf16),
        ((16, 80, 128), bf16), ((16, 80, 128), bf16), ((8, 160, 128), bf16), ((8, 160, 128), bf16),
        ((8, 10, 8, 128), f32), ((8, 10, 8, 128), f32), ((4, 8, 3, 8, 128), f32),
        ((4, 8, 3, 8, 128), f32), ((16, 8, 128), f32), ((16, 8, 128), f32), ((16, 8, 128), f32),
        ((2, 4, 10, 8, 128), f32), ((2, 4, 4, 3, 8, 128), f32),
        ((512, 512), bf16), ((512, 512), bf16), ((512, 256), bf16), ((256, 512), bf16),
        ((320, 320), bf16),
    ]
    embeds_llm, grad_a, grad_b = pl.pallas_call(
        block_kernel,
        out_shape=(
            jax.ShapeDtypeStruct((320, 512), bf16),
            jax.ShapeDtypeStruct((64, 1280), f32),
            jax.ShapeDtypeStruct((64, 1280), f32),
        ),
        in_specs=[pl.BlockSpec(memory_space=pl.ANY)] * 11,
        out_specs=(whole,) * 3,
        scratch_shapes=[pltpu.VMEM(shape, kind) for shape, kind in buffers]
        + [pltpu.SemaphoreType.DMA((count,)) for count in semaphores],
        compiler_params=pltpu.CompilerParams(
            collective_id=0, has_side_effects=True, vmem_limit_bytes=60 * 1024 * 1024
        ),
        name="block",
    )(
        first_weight,
        second_weight.T,
        patches.T,
        language_slot_gradient.T,
        routes.T,
        gain,
        shift,
        first_bias,
        second_bias,
        adapter_down.T,
        adapter_up,
    )
    return embeds_llm.T, grad_a.T, grad_b


def solution(mesh):
    placed = (
        P("dp", "mp"),
        P("dp", None),
        P(),
        P(),
        P("dp", "mp"),
        P("mp"),
        P(),
        P(None, "mp"),
        P("mp", "dp"),
        P("mp"),
        P("dp", "mp"),
    )
    return jax.shard_map(
        local,
        mesh=mesh,
        in_specs=placed,
        out_specs=(P("dp", "mp"), P(), P(None, "mp")),
        check_vma=False,
    )
```

```python
import math

import jax
import jax.numpy as jnp
from jax import lax
from jax.experimental import pallas as pl
from jax.experimental.pallas import tpu as pltpu
from jax.sharding import PartitionSpec as P

MESH = pl.DeviceIdType.MESH
X_CHIPS, Z_CHIPS, MP = 4, 16, 4
QUAD, HALF, OCT = 4, 8, 8
MATE_LAG, NEAR_LAG, FAR_LAG = 0, 1, 2
SLOT_STEPS = {HALF - 3: [1, 2, 3, 15, 14, 13], HALF - 2: [4, 5, 12, 11], HALF - 1: [6, 7, 10, 9, 8]}
TILES, SUM_TILES = 16, 13
GRAD_B_TILES, A_TILES = 10, 3
FAR_FIRST = sorted(range(1, Z_CHIPS), key=lambda offset: abs(offset - HALF))


def one_hot(places, count):
    columns = lax.broadcasted_iota(jnp.int32, (places.shape[0], count), 1)
    return (columns == places).astype(jnp.bfloat16)


def f32_dot(a, b):
    return jnp.dot(a, b, preferred_element_type=jnp.float32)


def f32_dot_t(a, b):
    return lax.dot_general(a, b, (((1,), (1,)), ((), ())), preferred_element_type=jnp.float32)


def pack(values, groups):
    values = values.reshape(groups, -1, 320)
    half = values.shape[1] // 2
    tail = jnp.concatenate([values[:, :half, 256:320], values[:, half:, 256:320]], axis=2)
    return jnp.concatenate([values[:, :, 0:128], values[:, :, 128:256], tail], axis=1)


def unpack(packed):
    groups, count = packed.shape[0], packed.shape[1] * 2 // 5
    tail = packed[:, 2 * count:]
    tail = jnp.concatenate([tail[:, :, 0:64], tail[:, :, 64:128]], axis=1)
    return jnp.concatenate(
        [packed[:, :count], packed[:, count:2 * count], tail], axis=2
    ).reshape(groups * count, 320)


def block_kernel(
    first_hbm, second_hbm, patches_hbm, slots_hbm, routes_hbm, gain_hbm, shift_hbm,
    first_bias_hbm, second_bias_hbm, down_hbm, up_hbm,
    embeds_ref, grad_a_ref, grad_b_ref,
    shards, patches_t, slots_t, routes_ref, gain_ref, shift_ref, first_bias_ref, second_bias_ref,
    down_ref, up_ref, pieces,
    weights, staged, rows, normed, grads, act, slope, partial, got_partial,
    in_a, in_b, in_c, in_e, out_a, out_b, out_c, out_e,
    parts_b, got_b, parts_a, got_a, reduced, got_tiles, total, whole_b, whole_a,
    regroup, ordered, placing, picking, same_features,
    quad_send, quad_recv, ring_send, ring_recv, near_send, near_recv, far_send, far_recv,
    mate_send, mate_recv, y_send, y_recv, z_send, z_recv, oct_send, oct_recv,
    wide_send, wide_recv, end_send, end_recv, load_sem,
):
    dp, y = lax.axis_index("dp"), lax.axis_index("mp")
    core = lax.rem(dp, 2)
    z = lax.rem(dp // 2, Z_CHIPS)
    x = dp // (2 * Z_CHIPS)
    turn = 1 - 2 * core
    own_oct = x * 2 + core

    def dp_of(x_at, z_at, core_at):
        return x_at * (2 * Z_CHIPS) + z_at * 2 + core_at

    z_turned = {d: lax.rem(z + turn * d + Z_CHIPS, Z_CHIPS) for d in range(-HALF, HALF + 1)}
    x_turned = {d: lax.rem(x + turn * d + X_CHIPS, X_CHIPS) for d in range(-2, 2)}
    x_blocks = {d: x_turned[d] * Z_CHIPS for d in x_turned}

    def block_at(x_step, z_step):
        return x_blocks[x_step] + z_turned[z_step]

    def row_places(count):
        return lax.broadcasted_iota(jnp.int32, (count, 1), 0)

    other_core = 1 - core
    cores = (core, other_core)
    lane = lax.rem(z, QUAD)
    quad_peers = []
    for step in range(QUAD):
        other = lax.rem(lane + step, QUAD)
        for flip in range(2):
            if step or flip:
                quad_peers.append((other, dp_of(x, z - lane + other, cores[flip])))
    ring_next = dp_of(x, z_turned[1], core)
    x_next = dp_of(x_turned[1], z, core)
    mate = dp_of(x, z, other_core)
    z_peers = [lax.rem(z + step, Z_CHIPS) for step in range(1, Z_CHIPS)]
    z_peer_dps = [dp_of(x, z_at, core) for z_at in z_peers]
    y_peers = [lax.rem(y + step, MP) for step in range(1, MP)]
    oct_peers = []
    for step in range(1, OCT):
        x_at, core_at = lax.rem(x + step // 2, X_CHIPS), cores[step % 2]
        oct_peers.append((x_at * 2 + core_at, dp_of(x_at, z, core_at)))

    wide_peers = []
    for y_step in range(MP):
        y_at = y_peers[y_step - 1] if y_step else y
        if y_step:
            wide_peers.append((y_at, own_oct, dp))
        wide_peers += [(y_at, at_oct, peer) for at_oct, peer in oct_peers]

    x_peers = [lax.rem(x + step, X_CHIPS) for step in range(1, X_CHIPS)]
    x_peer_dps = [dp_of(x_at, z, core) for x_at in x_peers]
    plane_peers = [(y, peer) for peer in x_peer_dps]
    plane_peers += [(y_at, peer) for y_at in y_peers for peer in [dp] + x_peer_dps]

    loads = [
        pltpu.make_async_copy(source, target, load_sem.at[at])
        for at, (source, target) in enumerate((
            (first_hbm, shards.at[0]), (second_hbm, shards.at[1]), (patches_hbm, patches_t),
            (slots_hbm, slots_t), (routes_hbm, routes_ref), (gain_hbm, gain_ref), (shift_hbm, shift_ref),
            (first_bias_hbm, first_bias_ref), (second_bias_hbm, second_bias_ref),
            (down_hbm, down_ref),
            (up_hbm, up_ref),
        ))
    ]
    for load in loads:
        load.start()

    barrier = pltpu.get_barrier_semaphore()
    greeted = [(peer, y) for _, peer in quad_peers]
    greeted += [(peer, y) for peer in z_peer_dps]
    greeted += [(peer, y_at) for y_at, _, peer in wide_peers]
    for peer in greeted:
        pl.semaphore_signal(barrier, inc=1, device_id=peer, device_id_type=MESH)
    for load in loads[:4]:
        load.wait()
    for weight in range(2):
        for half in range(2):
            pieces[2 * weight + half, 0:10] = shards[weight, :, 640 * half:640 * half + 640]
            pieces[2 * weight + half, 10:16] = jnp.zeros((6, 640), jnp.bfloat16)
    rows[y] = patches_t[...]
    pl.semaphore_wait(barrier, len(greeted))

    sent = []

    def send(source, target, send_sem, recv_sem, peer, peer_y=None):
        copy = pltpu.make_async_remote_copy(
            src_ref=source,
            dst_ref=target,
            send_sem=send_sem,
            recv_sem=recv_sem,
            device_id=(peer, y if peer_y is None else peer_y),
            device_id_type=MESH,
        )
        copy.start()
        sent.append(copy)
        return copy

    def wait_all(copies):
        for copy in copies:
            copy.wait_recv()

    def to_y(buffer, phase):
        return [
            send(buffer.at[y], buffer.at[y], y_send.at[3 * phase + at], y_recv.at[3 * phase + at],
                 dp, y_at)
            for at, y_at in enumerate(y_peers)
        ]

    def to_one_z(source, target, phase, offset):
        z_at, at = z_peers[offset - 1], 15 * phase + offset - 1
        return send(source.at[z_at], target.at[z], z_send.at[at], z_recv.at[at],
                    z_peer_dps[offset - 1])

    def to_z(source, target, phase):
        return [to_one_z(source, target, phase, offset) for offset in FAR_FIRST]

    def to_oct(source_of, target, phase):
        first = 7 * phase
        return [
            send(source_of(at_oct), target, oct_send.at[first + at], oct_recv.at[first + at], peer)
            for at, (at_oct, peer) in enumerate(oct_peers)
        ]

    def to_wide(source_of, target, phase):
        first = 31 * phase
        return [
            send(source_of(y_at, at_oct), target, wide_send.at[first + at],
                 wide_recv.at[first + at], peer, y_at)
            for at, (y_at, at_oct, peer) in enumerate(wide_peers)
        ]

    def block_copy(block, sends, recvs, at, peer):
        return pltpu.make_async_remote_copy(
            src_ref=weights.at[block],
            dst_ref=weights.at[block],
            send_sem=sends.at[at],
            recv_sem=recvs.at[at],
            device_id=(peer, y),
            device_id_type=MESH,
        )

    def send_block(block, sends, recvs, at, peer):
        copy = block_copy(block, sends, recvs, at, peer)
        copy.start()
        sent.append(copy)

    def ring_part(block, part, step):
        rows_of = pl.ds(48 * part, 48 - 16 * part)
        return pltpu.make_async_remote_copy(
            src_ref=weights.at[block, rows_of],
            dst_ref=weights.at[block, rows_of],
            send_sem=ring_send.at[2 * step + part],
            recv_sem=ring_recv.at[2 * step + part],
            device_id=(ring_next, y),
            device_id_type=MESH,
        )

    def send_ring_part(block, part, step):
        copy = ring_part(block, part, step)
        copy.start()
        sent.append(copy)

    def arrived(block, sends, recvs, at):
        block_copy(block, sends, recvs, at, mate).wait_recv()

    def regroup_for_oct(received):
        moved = f32_dot(regroup[...], unpack(received[...]))
        return pack(moved.astype(jnp.bfloat16), OCT)

    own = lane * 2 + core
    swaps = [
        send(pieces.at[other], staged.at[own], quad_send.at[at], quad_recv.at[at], peer)
        for at, (other, peer) in enumerate(quad_peers)
    ]
    row_copies = to_y(rows, 0)
    staged[own] = pieces[lane]

    n = row_places(512)
    place = (n // 8 % 4) * 128 + (n // 32) * 8 + n % 8
    moved = f32_dot_t(one_hot(place, 512), slots_t[...])
    in_a[...] = pack(moved.astype(jnp.bfloat16), Z_CHIPS)
    in_b[z] = in_a[z]
    slot_copies = []

    wait_all(swaps)
    n = row_places(80)
    mine = block_at(0, 0)
    weights[mine] = f32_dot(
        one_hot(n // 10 * 16 + n % 10, 128), staged[...].reshape(128, 640)
    ).astype(jnp.bfloat16)

    latents, places = [], []
    same = one_hot(row_places(256), 256)

    def as_row(vector):
        return vector[...].astype(jnp.float32).reshape(1, vector.shape[0])

    def down_of(j):
        return down_ref[:, 320 * j:320 * j + 320]

    def up_of(half):
        return up_ref[:, 640 * half:640 * half + 640]

    def find_places():
        at_row = lax.broadcasted_iota(jnp.int32, (256, 256), 0)
        at_column = lax.broadcasted_iota(jnp.int32, (256, 256), 1)
        wide = jnp.where(at_row == at_column, routes_ref[...], 0).astype(jnp.float32)
        routes = jnp.sum(wide, axis=1, keepdims=True).astype(jnp.int32)
        hits = one_hot(routes, 128)
        before = f32_dot((at_column < at_row).astype(jnp.bfloat16), hits)
        rank_in = jnp.sum(before * hits.astype(jnp.float32), axis=1, keepdims=True)
        rank_in = rank_in.astype(jnp.int32)
        x_to, z_to, core_to = routes // 32, routes // 2 % 16, routes % 2
        place_out = z_to * 32 + x_to * 8 + core_to * 4 + rank_in
        wide = jnp.where(at_row == at_column, place_out, 0).astype(jnp.float32)
        places.append(jnp.sum(wide, axis=0, keepdims=True).astype(jnp.int32))
        places.append(x_to * 128 + core_to * 64 + z_to * 4 + rank_in)

    def norm_rows():
        for load in loads[4:]:
            load.wait()
        find_places()
        wait_all(row_copies)
        gain, shift = as_row(gain_ref), as_row(shift_ref)
        floats = [f32_dot_t(same, rows[j]) for j in range(MP)]
        mean = sum(jnp.sum(f, axis=-1, keepdims=True) for f in floats) * (1.0 / 1280)
        centred = [f - mean for f in floats]
        var = sum(jnp.sum(c * c, axis=-1, keepdims=True) for c in centred) * (1.0 / 1280)
        scale = lax.rsqrt(var + 1e-06)
        for j in range(MP):
            features = slice(320 * j, 320 * j + 320)
            normed[j] = (centred[j] * scale * gain[:, features] + shift[:, features]).astype(
                jnp.bfloat16
            )
        latents.append(
            sum(f32_dot_t(normed[j], down_of(j)) for j in range(MP)).astype(jnp.bfloat16)
        )
        latents.append(
            sum(f32_dot_t(down_of(j), normed[j]) for j in range(MP)).astype(jnp.bfloat16)
        )

    slot_steps = []

    def make_moves():
        n = row_places(512)
        regroup[...] = one_hot((n // 4 % 16) * 32 + (n // 64) * 4 + n % 4, 512)
        ordered[...] = one_hot(
            (n // 128) * 128 + (n // 4 % 2) * 64 + (n // 8 % 16) * 4 + n % 4, 512
        )
        placing[...] = (n == places[0]).astype(jnp.bfloat16)
        picking[...] = one_hot(places[1], 512)
        same_features[...] = one_hot(row_places(320), 320)

    def slots_to_oct():
        wait_all(slot_copies)
        in_c[...] = regroup_for_oct(in_b)
        in_e[own_oct] = in_c[own_oct]
        slot_steps.append(to_oct(lambda o: in_c.at[o], in_e.at[own_oct], 0))

    def pick_grads():
        wait_all(slot_steps[0])
        picked = f32_dot(picking[...], unpack(in_e[...])).astype(jnp.bfloat16)
        grads[y] = f32_dot_t(same_features[...], picked).astype(jnp.bfloat16)
        slot_steps.append(to_y(grads, 1))

    between = {3: [norm_rows], 6: [make_moves]}

    for step in range(HALF + 1 + FAR_LAG):
        if step <= HALF:
            first = block_at(0, -step)
            if step:
                for part in range(2):
                    ring_part(first, part, step - 1).wait_recv()
                    if step < HALF:
                        send_ring_part(first, part, step)
            else:
                send_ring_part(first, 0, step)
                send_ring_part(first, 1, step)
            send_block(first, near_send, near_recv, 2 * step if step < HALF else 15, x_next)
            if 0 < step < HALF:
                send_block(first, mate_send, mate_recv, step, mate)
        if 0 < step - MATE_LAG < HALF:
            before = step - MATE_LAG
            second = block_at(0, before)
            arrived(second, mate_send, mate_recv, before)
            send_block(second, near_send, near_recv, 2 * before - 1, x_next)
        if step in SLOT_STEPS:
            for offset in SLOT_STEPS[step]:
                slot_copies.append(to_one_z(in_a, in_b, 0, offset))
        before = step - NEAR_LAG
        if 0 <= before <= HALF:
            at = 2 * before if before < HALF else 15
            block = block_at(-1, -before)
            arrived(block, near_send, near_recv, at)
            if before == 0:
                @pl.when(core == 0)
                def _():
                    block_copy(block, far_send, far_recv, 0, x_next).start()
            elif before == HALF:
                @pl.when(core == 1)
                def _():
                    block_copy(block, far_send, far_recv, 0, x_next).start()
            else:
                send_block(block, far_send, far_recv, before, x_next)
            send_block(block, mate_send, mate_recv, 8 + at, mate)
            if 0 < before < HALF:
                block = block_at(-1, before)
                arrived(block, near_send, near_recv, 2 * before - 1)
                send_block(block, mate_send, mate_recv, 8 + 2 * before - 1, mate)
        before = step - FAR_LAG
        if 0 < before < HALF:
            block = block_at(-2, -before)
            arrived(block, far_send, far_recv, before)
            send_block(block, mate_send, mate_recv, 24 + before, mate)
        for job in between.get(step, ()):
            job()
    block = x_blocks[-2] + lax.rem(z + HALF * core, Z_CHIPS)
    arrived(block, far_send, far_recv, 0)
    send_block(block, mate_send, mate_recv, 24, mate)
    for at in range(8, 32):
        arrived(mine, mate_send, mate_recv, at)

    latent, latent_t = latents
    first_bias = as_row(first_bias_ref)

    def first_block(j, half):
        return jnp.concatenate([weights[j * 16 + quad * 4 + half] for quad in range(4)], 0)

    def second_block(j, half):
        return jnp.concatenate([weights[j * 16 + quad * 4 + 2 + half] for quad in range(4)], 0)

    for half in range(2):
        pre = sum(f32_dot(normed[j], first_block(j, half)) for j in range(MP))
        pre = pre + f32_dot(latent, up_of(half)) + first_bias[:, 640 * half:640 * half + 640]
        sigma = jax.nn.sigmoid(1.702 * pre)
        act[half] = (pre * sigma).astype(jnp.bfloat16)
        slope[half] = sigma + 1.702 * pre * sigma * (1.0 - sigma)
    partial_copies = []
    for step in (2, 1, 3, 0):
        y_at = lax.rem(y + step, MP)
        partial[step] = sum(
            f32_dot_t(second_block(y_at, half), act[half]) for half in range(2)
        ).astype(jnp.bfloat16)
        if step:
            partial_copies.append(
                send(partial.at[step], got_partial.at[step - 1], y_send.at[5 + step],
                     y_recv.at[5 + step], dp, y_at)
            )

    slots_to_oct()
    pick_grads()

    wait_all(partial_copies)
    branch = partial[0].astype(jnp.float32)
    for at in range(3):
        branch = branch + got_partial[at].astype(jnp.float32)
    at_row = lax.broadcasted_iota(jnp.int32, (320, 320), 0)
    at_column = lax.broadcasted_iota(jnp.int32, (320, 320), 1)
    bias = jnp.sum(
        jnp.where(at_row == at_column, as_row(second_bias_ref), 0.0), axis=1, keepdims=True
    )
    embeds = (patches_t[...].astype(jnp.float32) + branch + bias).astype(jnp.bfloat16)
    out_a[...] = pack(f32_dot_t(placing[...], embeds).astype(jnp.bfloat16), Z_CHIPS)
    out_b[z] = out_a[z]
    out_copies = to_z(out_a, out_b, 1)

    wait_all(slot_steps[1])
    grad_rows = [f32_dot_t(same, grads[j]).astype(jnp.bfloat16) for j in range(MP)]
    lora_t = jnp.zeros((64, 256), jnp.float32)
    for half in range(2):
        grad_act = sum(f32_dot(grad_rows[j], second_block(j, half)) for j in range(MP))
        grad_pre = (grad_act * slope[half]).astype(jnp.bfloat16)
        lora_t = lora_t + f32_dot_t(up_of(half), grad_pre)
        grad_b = f32_dot(latent_t, grad_pre)
        for o in range(OCT):
            for tile in range(5):
                parts_b[o, half * 5 + tile] = grad_b[8 * o:8 * o + 8, 128 * tile:128 * tile + 128]
    got_b[own_oct] = parts_b[own_oct]
    b_copies = to_oct(lambda o: parts_b.at[o], got_b.at[own_oct], 1)

    tops = []
    for _ in range(3):
        tops.append(lora_t.astype(jnp.bfloat16))
        lora_t = lora_t - tops[-1].astype(jnp.float32)
    grad_a = jnp.concatenate(
        [sum(f32_dot(top, normed[j]) for top in tops) for j in range(MP)], axis=1
    )
    for tile in range(MP * A_TILES):
        for o in range(OCT):
            strip = (
                grad_a[8 * o:8 * o + 8, 128 * tile:128 * tile + 128]
                if tile < GRAD_B_TILES
                else jnp.zeros((8, 128), jnp.float32)
            )
            parts_a[tile // A_TILES, o, tile % A_TILES] = strip
    got_a[y, own_oct] = parts_a[y, own_oct]
    a_copies = to_wide(lambda y_at, o: parts_a.at[y_at, o], got_a.at[y, own_oct], 0)

    wait_all(b_copies)
    reduced[0:GRAD_B_TILES] = jnp.sum(got_b[...], axis=0)
    wait_all(a_copies)
    reduced[GRAD_B_TILES:SUM_TILES] = jnp.sum(got_a[...], axis=(0, 1))
    reduced[SUM_TILES:TILES] = jnp.zeros((TILES - SUM_TILES, 8, 128), jnp.float32)
    got_tiles[z] = reduced[z]
    tile_copies = to_z(reduced, got_tiles, 2)

    wait_all(out_copies)
    out_c[...] = regroup_for_oct(out_b)
    out_e[own_oct] = out_c[own_oct]
    oct_copies = to_oct(lambda o: out_c.at[o], out_e.at[own_oct], 2)

    wait_all(tile_copies)
    total[z] = jnp.sum(got_tiles[...], axis=0) * (1.0 / math.sqrt(32768))
    total_copies = [
        send(total.at[z], total.at[z], z_send.at[45 + at], z_recv.at[45 + at], peer)
        for at, peer in ((offset - 1, z_peer_dps[offset - 1]) for offset in FAR_FIRST)
    ]

    wait_all(total_copies)
    whole_b[core, x] = total[0:GRAD_B_TILES]
    whole_a[core, y, x] = total[GRAD_B_TILES:SUM_TILES]
    b_target, a_target = whole_b.at[core, x], whole_a.at[core, y, x]
    whole_copies = [
        send(total.at[pl.ds(0, GRAD_B_TILES)], b_target, end_send.at[at], end_recv.at[at], peer)
        for at, peer in enumerate(x_peer_dps)
    ]
    whole_copies += [
        send(total.at[pl.ds(GRAD_B_TILES, A_TILES)], a_target, end_send.at[3 + at],
             end_recv.at[3 + at], peer, y_at)
        for at, (y_at, peer) in enumerate(plane_peers)
    ]

    wait_all(whole_copies)
    mate_copies = [
        send(whole.at[core], whole.at[core], end_send.at[18 + at], end_recv.at[18 + at], mate)
        for at, whole in enumerate((whole_b, whole_a))
    ]
    wait_all(oct_copies)
    embeds_ref[...] = f32_dot(ordered[...], unpack(out_e[...])).T.astype(jnp.bfloat16)
    wait_all(mate_copies)
    for o in range(OCT):
        for tile in range(GRAD_B_TILES):
            grad_b_ref[8 * o:8 * o + 8, 128 * tile:128 * tile + 128] = whole_b[
                o % 2, o // 2, tile
            ]
    for tile in range(GRAD_B_TILES):
        for o in range(OCT):
            grad_a_ref[8 * o:8 * o + 8, 128 * tile:128 * tile + 128] = whole_a[
                o % 2, tile // A_TILES, o // 2, tile % A_TILES
            ]

    block_copy(mine, far_send, far_recv, 0, x_next).wait_send()
    for copy in sent:
        copy.wait_send()


def local(
    patches,
    routes,
    gain,
    shift,
    first_weight,
    first_bias,
    adapter_down,
    adapter_up,
    second_weight,
    second_bias,
    language_slot_gradient,
):
    bf16, f32 = jnp.bfloat16, jnp.float32
    whole = pl.BlockSpec(memory_space=pltpu.VMEM)
    semaphores = [7, 7, 16, 16, 16, 16, 8, 8, 32, 32, 9, 9, 60, 60, 21, 21, 31, 31, 20, 20, 11]
    buffers = [
        ((2, 10, 1280), bf16), ((320, 256), bf16), ((320, 512), bf16), ((1, 256), jnp.int32),
        ((1280,), bf16), ((1280,), bf16), ((1280,), bf16), ((320,), bf16),
        ((64, 1280), bf16), ((64, 1280), bf16),
        ((4, 16, 640), bf16),
        ((64, 80, 640), bf16), ((8, 16, 640), bf16), ((4, 320, 256), bf16), ((4, 256, 320), bf16),
        ((4, 320, 256), bf16), ((2, 256, 640), bf16), ((2, 256, 640), f32), ((4, 320, 256), bf16),
        ((3, 320, 256), bf16),
        ((16, 80, 128), bf16), ((16, 80, 128), bf16), ((8, 160, 128), bf16), ((8, 160, 128), bf16),
        ((16, 80, 128), bf16), ((16, 80, 128), bf16), ((8, 160, 128), bf16), ((8, 160, 128), bf16),
        ((8, 10, 8, 128), f32), ((8, 10, 8, 128), f32), ((4, 8, 3, 8, 128), f32),
        ((4, 8, 3, 8, 128), f32), ((16, 8, 128), f32), ((16, 8, 128), f32), ((16, 8, 128), f32),
        ((2, 4, 10, 8, 128), f32), ((2, 4, 4, 3, 8, 128), f32),
        ((512, 512), bf16), ((512, 512), bf16), ((512, 256), bf16), ((256, 512), bf16),
        ((320, 320), bf16),
    ]
    embeds_llm, grad_a, grad_b = pl.pallas_call(
        block_kernel,
        out_shape=(
            jax.ShapeDtypeStruct((320, 512), bf16),
            jax.ShapeDtypeStruct((64, 1280), f32),
            jax.ShapeDtypeStruct((64, 1280), f32),
        ),
        in_specs=[pl.BlockSpec(memory_space=pl.ANY)] * 11,
        out_specs=(whole,) * 3,
        scratch_shapes=[pltpu.VMEM(shape, kind) for shape, kind in buffers]
        + [pltpu.SemaphoreType.DMA((count,)) for count in semaphores],
        compiler_params=pltpu.CompilerParams(
            collective_id=0, has_side_effects=True, vmem_limit_bytes=60 * 1024 * 1024
        ),
        name="block",
    )(
        first_weight,
        second_weight.T,
        patches.T,
        language_slot_gradient.T,
        routes.T,
        gain,
        shift,
        first_bias,
        second_bias,
        adapter_down.T,
        adapter_up,
    )
    return embeds_llm.T, grad_a.T, grad_b


def solution(mesh):
    placed = (
        P("dp", "mp"),
        P("dp", None),
        P(),
        P(),
        P("dp", "mp"),
        P("mp"),
        P(),
        P(None, "mp"),
        P("mp", "dp"),
        P("mp"),
        P("dp", "mp"),
    )
    return jax.shard_map(
        local,
        mesh=mesh,
        in_specs=placed,
        out_specs=(P("dp", "mp"), P(), P(None, "mp")),
        check_vma=False,
    )
```
